32 devices in a mesh: users: 8 (over y, x, core), items: 4 (over z).
Axes of the slice: x: 2, y: 2, z: 4, core: 2. Of those that a mesh axis runs over, the one named last changes fastest.
Arguments:
- tiles: float32 [8, 4, 4, 32, 128, 128], P('users', 'items'), may hold values from -6 to 6
- user_blocks: int32 [8, 4, 4], P('users', 'items'), may hold values from 0 to 15, as said below
- item_blocks: int32 [8, 4, 4], P('users', 'items'), may hold values from 0 to 127, as said below
- counts: int32 [8, 4], P('users', 'items'), may hold values from 1 to 4, as said below
- user_factor: float32 [64, 16384], P(None, ('users', 'items')), may hold values from -0.5 to 0.5
- item_factor: float32 [64, 65536], P(None, ('items', 'users')), may hold values from -0.5 to 0.5
- week_factor: float32 [32, 64], replicated, may hold values from -1 to 1
Outputs:
- m_users: float32 [64, 16384], P(None, ('users', 'items'))
- m_items: float32 [64, 65536], P(None, ('items', 'users'))
The draws below stay inside these ranges and needn't reach their ends.
Inputs may be any that keep to these rules, and one draw needn't show every extreme that they name: `user_blocks`: within one device the first 4 slots name distinct (user block, item block) pairs of its grid row and grid column. `item_blocks`: paired with user_blocks slot by slot. `counts`: some device holds 4 tiles in every draw.
All inputs are finite; a program needn't handle non-finite values.
Results may differ from the reference program's by a relative error of at most 0.0001.
Values sent between devices are 32-bit elements; how exact they have to be, the bound alone decides.
No kernel may reach another device: no remote copies, remote signals or barrier semaphores. Data moves between devices by JAX's collectives and lax.ppermute only.
A program may use at most 128 MiB of HBM per device.

```python
import jax
import jax.numpy as jnp
from jax import lax

BU = 128
BI = 128
WEEKS = 32
RANK = 64
UBD = 16
IBD = 128
SLOTS = 4
USER_ROWS = 16384
ITEM_ROWS = 65536
N_USERS = 8
N_ITEMS = 4


def tile_layout(key):
    devices = N_USERS * N_ITEMS
    cells = UBD * IBD
    keys = jax.random.split(jax.random.fold_in(key, 11), devices)
    orders = jax.vmap(lambda sub_key: jax.random.permutation(sub_key, cells))(keys)[:, :SLOTS]
    orders = orders.astype(jnp.int32)
    picked = jax.random.randint(jax.random.fold_in(key, 12), (), 0, devices)
    second = (picked + 1) % devices
    rows = jnp.arange(devices, dtype=jnp.int32)[:, None]
    columns = jnp.arange(SLOTS, dtype=jnp.int32)[None, :]
    last_cell = cells - 1
    moved = jnp.where(orders == last_cell, orders[:, 0:1], orders)
    orders = jnp.where(rows == picked, jnp.where(columns == 0, last_cell, moved), orders)
    moved = jnp.where(orders == 0, orders[:, 0:1], orders)
    orders = jnp.where(rows == second, jnp.where(columns == 0, 0, moved), orders)
    return orders.reshape(N_USERS, N_ITEMS, SLOTS)


def draw_user_blocks(key, part):
    return (tile_layout(key) // IBD).astype(jnp.int32)


def draw_item_blocks(key, part):
    return (tile_layout(key) % IBD).astype(jnp.int32)


def draw_counts(key, part):
    devices = N_USERS * N_ITEMS
    upper = max(SLOTS // 2, 1) + 1
    base = jax.random.randint(jax.random.fold_in(key, 21), (devices,), 1, upper)
    filled = jax.random.randint(jax.random.fold_in(key, 22), (devices,), 0, 8) == 0
    picked = jax.random.randint(jax.random.fold_in(key, 23), (), 0, devices)
    filled = filled | (jnp.arange(devices, dtype=jnp.int32) == picked)
    return jnp.where(filled, SLOTS, base).astype(jnp.int32).reshape(N_USERS, N_ITEMS)


def level_of(rng, shape, shards, low, top_value):
    gain, own = 1.0, jax.random.fold_in(rng, 6)
    for dim, parts in shards:
        steps = jnp.exp(jax.random.uniform(jax.random.fold_in(own, dim), (parts,), jnp.float32, low / len(shards), top_value / len(shards)))
        gain = gain * jnp.repeat(steps, shape[dim] // parts).reshape([-1 if axis == dim else 1 for axis in range(len(shape))])
    return gain


def centred(stream_key, extent, spread, bound, shards=(), held_as=jnp.bfloat16):
    array = spread * jax.random.normal(stream_key, extent, jnp.float32)
    if shards:
        array = array * level_of(stream_key, extent, shards, -0.22, 0.18)
    return jnp.clip(array, -bound, bound).astype(held_as)


def setup_inputs(seed: int = 0) -> dict:
    splits = jax.random.split(jax.random.key(seed), 8)
    return {
        "tiles": centred(splits[0], (N_USERS, N_ITEMS, SLOTS, WEEKS, BU, BI), 1.0, 6.0, ((0, 8), (1, 4)), jnp.float32),
        "user_blocks": draw_user_blocks(jax.random.fold_in(splits[7], 71), 0),
        "item_blocks": draw_item_blocks(jax.random.fold_in(splits[7], 71), 0),
        "counts": draw_counts(jax.random.fold_in(splits[7], 71), 0),
        "user_factor": centred(splits[4], (RANK, USER_ROWS), BU ** -0.5, 0.5, ((1, 32),), jnp.float32),
        "item_factor": centred(splits[5], (RANK, ITEM_ROWS), BI ** -0.5, 0.5, ((1, 32),), jnp.float32),
        "week_factor": centred(splits[6], (WEEKS, RANK), WEEKS ** -0.5, 1.0, (), jnp.float32),
    }


def reference(tiles, user_blocks, item_blocks, counts, user_factor, item_factor, week_factor):
    total = N_USERS * N_ITEMS * SLOTS
    flat_tiles = tiles.reshape(total, WEEKS, BU, BI)
    order = jnp.arange(total, dtype=jnp.int32)
    device_index = order // SLOTS
    slot_index = order % SLOTS
    grid_row = device_index // N_ITEMS
    grid_column = device_index % N_ITEMS
    live = slot_index < counts.reshape(-1)[device_index]
    user_start = ((grid_row * UBD + user_blocks.reshape(-1)) * BU).astype(jnp.int32)
    item_start = ((grid_column * IBD + item_blocks.reshape(-1)) * BI).astype(jnp.int32)
    highest = lax.Precision.HIGHEST

    def accumulate(sums_pair, packed):
        tile_data, user_at, item_at, tile_live = packed
        user_block = lax.dynamic_slice_in_dim(user_factor, user_at, BU, 1)
        item_block = lax.dynamic_slice_in_dim(item_factor, item_at, BI, 1)
        weekly = jnp.einsum('kr,kab->rab', week_factor, tile_data, precision=highest)
        scale = tile_live.astype(weekly.dtype)
        user_term = jnp.einsum('rab,rb->ra', weekly, item_block, precision=highest) * scale
        item_term = jnp.einsum('rab,ra->rb', weekly, user_block, precision=highest) * scale
        users_sum = lax.dynamic_update_slice_in_dim(
            sums_pair[0], lax.dynamic_slice_in_dim(sums_pair[0], user_at, BU, 1) + user_term, user_at, 1)
        items_sum = lax.dynamic_update_slice_in_dim(
            sums_pair[1], lax.dynamic_slice_in_dim(sums_pair[1], item_at, BI, 1) + item_term, item_at, 1)
        return (users_sum, items_sum), None

    start_pair = (jnp.zeros((RANK, USER_ROWS), jnp.float32), jnp.zeros((RANK, ITEM_ROWS), jnp.float32))
    (m_users, m_items), _ = lax.scan(accumulate, start_pair, (flat_tiles, user_start, item_start, live))
    return (m_users, m_items)
```

```python
import functools

import jax
import jax.numpy as jnp
from jax import lax
from jax.experimental import pallas as pl
from jax.experimental.pallas import tpu as pltpu
from jax.sharding import PartitionSpec as P

F32 = jnp.float32
BF16 = jnp.bfloat16
ANY = pl.BlockSpec(memory_space=pl.ANY)
SMEM = pl.BlockSpec(memory_space=pltpu.SMEM)
VMEM = pl.BlockSpec(memory_space=pltpu.VMEM)


def columns(block, width):
    return pl.ds(pl.multiple_of(block * width, width), width)


def split(value):
    high = value.astype(BF16)
    return high, (value - high.astype(F32)).astype(BF16)


def serve_kernel(chips, slots, width, *refs):
    requests = refs[: chips - 1]
    own, sibling = refs[chips - 1 : chips + 1]
    messages = refs[chips + 1 : 2 * chips]
    sems = refs[2 * chips]
    me = lax.axis_index("users")
    per_device = own.shape[1] // width
    todo = []
    for step in range(chips - 1):
        for slot in range(slots):
            index = requests[step][slot]
            device = index // per_device
            block = index % per_device
            target = messages[step].at[:, pl.ds(slot * width, width)]
            todo.append((device, block, target, sems.at[step, slot]))
    for device, block, target, sem in todo:
        for owner, source in ((me, own), (me ^ 1, sibling)):

            @pl.when(device == owner)
            def _():
                pltpu.make_async_copy(source.at[:, columns(block, width)], target, sem).start()

    for device, block, target, sem in todo:

        @pl.when(device // 2 == me // 2)
        def _():
            pltpu.make_async_copy(own.at[:, pl.ds(0, width)], target, sem).wait()


def spread_weeks(weeks_t, spread):
    for week in range(spread.shape[0]):
        spread[week] = jnp.broadcast_to(weeks_t[:, week : week + 1], spread.shape[1:])


def mode2_kernel(groups, *refs):
    count_ref, blocks_ref, weeks_t = refs[:3]
    factors = refs[3 : 3 + groups]
    tiles, terms, held, gathered, spread, tile_sems, block_sems = refs[3 + groups :]
    slots, weeks, height, width = tiles.shape
    rank = gathered.shape[1]
    me = lax.axis_index("items")
    count = count_ref[0, 0]
    per_device = factors[0].shape[1] // height
    for slot in range(slots):

        @pl.when(slot < count)
        def _():
            pltpu.make_async_copy(tiles.at[slot], held.at[slot], tile_sems.at[slot]).start()
            block = blocks_ref[slot]
            for step in range(groups):

                @pl.when(((block // per_device) ^ me) == step)
                def _():
                    pltpu.make_async_copy(
                        factors[step].at[:, columns(block % per_device, height)],
                        gathered.at[slot],
                        block_sems.at[slot],
                    ).start()

    spread_weeks(weeks_t, spread)
    terms[...] = jnp.zeros_like(terms)

    def work(slot, carry):
        pltpu.make_async_copy(tiles.at[slot], held.at[slot], tile_sems.at[slot]).wait()
        pltpu.make_async_copy(
            factors[0].at[:, pl.ds(0, height)], gathered.at[slot], block_sems.at[slot]
        ).wait()
        users = gathered[slot]
        total = jnp.zeros((2 * rank, 2 * width), F32)
        for week in range(0, weeks, 2):
            left, right = [], []
            for part in (week, week + 1):
                left.append(jnp.concatenate(split(spread[part] * users), axis=0))
                right.append(jnp.concatenate(split(held[slot, part]), axis=1))
            total += jnp.dot(
                jnp.concatenate(left, axis=1),
                jnp.concatenate(right, axis=0),
                preferred_element_type=F32,
            )
        half = total[:rank] + total[rank:]
        terms[:, columns(slot, width)] = half[:, :width] + half[:, width:]
        return carry

    lax.fori_loop(0, count, work, 0)


def mode1_kernel(groups, chips, *refs):
    count_ref, users_ref, items_ref, weeks_t, own, sibling = refs[:6]
    messages = refs[6 : 5 + chips]
    tiles = refs[5 + chips]
    parts = refs[6 + chips : 6 + chips + groups]
    held, gathered, spread, sums, tile_sems, block_sems = refs[6 + chips + groups :]
    slots, weeks, height, width = tiles.shape
    rank = gathered.shape[1]
    me = lax.axis_index("users")
    column = lax.axis_index("items")
    count = count_ref[0, 0]
    per_device = own.shape[1] // width
    for slot in range(slots):

        @pl.when(slot < count)
        def _():
            pltpu.make_async_copy(tiles.at[slot], held.at[slot], tile_sems.at[slot]).start()
            index = items_ref[slot]
            device = index // per_device
            block = index % per_device
            for owner, source in ((me, own), (me ^ 1, sibling)):

                @pl.when(device == owner)
                def _():
                    pltpu.make_async_copy(
                        source.at[:, columns(block, width)],
                        gathered.at[slot],
                        block_sems.at[slot],
                    ).start()

            for step in range(1, chips):

                @pl.when(((device // 2) ^ (me // 2)) == step)
                def _():
                    pltpu.make_async_copy(
                        messages[step - 1].at[:, pl.ds(slot * width, width)],
                        gathered.at[slot],
                        block_sems.at[slot],
                    ).start()

    spread_weeks(weeks_t, spread)
    sums[...] = jnp.zeros_like(sums)

    def work(slot, carry):
        pltpu.make_async_copy(tiles.at[slot], held.at[slot], tile_sems.at[slot]).wait()
        pltpu.make_async_copy(
            own.at[:, pl.ds(0, width)], gathered.at[slot], block_sems.at[slot]
        ).wait()
        items = gathered[slot]
        total = jnp.zeros((2 * rank, 2 * height), F32)
        for week in range(0, weeks, 2):
            left, right = [], []
            for part in (week, week + 1):
                left.append(jnp.concatenate(split(spread[part] * items), axis=0))
                right.append(jnp.concatenate(split(held[slot, part]), axis=0))
            total += lax.dot_general(
                jnp.concatenate(left, axis=1),
                jnp.concatenate(right, axis=1),
                (((1,), (1,)), ((), ())),
                preferred_element_type=F32,
            )
        half = total[:rank] + total[rank:]
        sums[users_ref[slot]] += half[:, :height] + half[:, height:]
        return carry

    lax.fori_loop(0, count, work, 0)
    kept = parts[0].shape[1] // height
    for step in range(groups):
        first = (column ^ step) * kept
        for block in range(kept):
            parts[step][:, block * height : (block + 1) * height] = sums[first + block]


def collect_kernel(chips, slots, width, *refs):
    requests = refs[: 2 * chips]
    terms = refs[2 * chips : 4 * chips]
    out, landed, sems = refs[4 * chips :]
    per_device = out.shape[1] // width
    me = lax.axis_index("users")
    todo = []
    for step in range(2 * chips):
        for slot in range(slots):
            index = requests[step][slot]
            todo.append((step, slot, index // per_device == me, index % per_device))
    for step, slot, mine, block in todo:

        @pl.when(mine)
        def _():
            pltpu.make_async_copy(
                terms[step].at[:, pl.ds(slot * width, width)],
                landed.at[step, slot],
                sems.at[step, slot],
            ).start()

    out[...] = jnp.zeros_like(out)
    for step, slot, mine, block in todo:

        @pl.when(mine)
        def _():
            pltpu.make_async_copy(
                terms[step].at[:, pl.ds(slot * width, width)],
                landed.at[step, slot],
                sems.at[step, slot],
            ).wait()
            out[:, columns(block, width)] += landed[step, slot]


def on_device(sizes, tiles, user_blocks, item_blocks, counts, user_factor, item_factor, week_factor):
    rows, groups = sizes
    chips = rows // 2
    tiles = tiles[0, 0]
    slots, weeks, height, width = tiles.shape
    rank = week_factor.shape[1]
    wanted_users = user_blocks[0, 0]
    wanted_items = item_blocks[0, 0]
    weeks_t = week_factor.T

    def across_chips(value, step):
        return lax.ppermute(value, "users", [(i, i ^ (2 * step)) for i in range(rows)])

    def across_cores(value):
        return lax.ppermute(value, "users", [(i, i ^ 1) for i in range(rows)])

    def across_groups(value, step):
        return lax.ppermute(value, "items", [(i, i ^ step) for i in range(groups)])

    requests = [across_chips(wanted_items, step) for step in range(1, chips)]
    sibling = across_cores(item_factor)
    row_factors = [user_factor] + [across_groups(user_factor, s) for s in range(1, groups)]
    near = [wanted_items] + requests
    far = [across_cores(value) for value in near]

    block = jax.ShapeDtypeStruct((rank, slots * width), F32)
    messages = pl.pallas_call(
        functools.partial(serve_kernel, chips, slots, width),
        out_shape=[block] * (chips - 1),
        in_specs=[SMEM] * (chips - 1) + [ANY] * 2,
        out_specs=[ANY] * (chips - 1),
        scratch_shapes=[pltpu.SemaphoreType.DMA((chips - 1, slots))],
        name="serve",
    )(*requests, item_factor, sibling)
    messages = [across_chips(m, step + 1) for step, m in enumerate(messages)]

    vmem_limit = 40 << 20
    terms = pl.pallas_call(
        functools.partial(mode2_kernel, groups),
        out_shape=block,
        in_specs=[SMEM] * 2 + [VMEM] + [ANY] * (groups + 1),
        out_specs=VMEM,
        scratch_shapes=[
            pltpu.VMEM((slots, weeks, height, width), F32),
            pltpu.VMEM((slots, rank, height), F32),
            pltpu.VMEM((weeks, rank, height), F32),
            pltpu.SemaphoreType.DMA((slots,)),
            pltpu.SemaphoreType.DMA((slots,)),
        ],
        compiler_params=pltpu.CompilerParams(vmem_limit_bytes=vmem_limit),
        name="mode2",
    )(counts, wanted_users, weeks_t, *row_factors, tiles)
    near_terms = [terms] + [across_chips(terms, step) for step in range(1, chips)]
    far_terms = [across_cores(value) for value in near_terms]

    user_width = user_factor.shape[1]
    parts = pl.pallas_call(
        functools.partial(mode1_kernel, groups, chips),
        out_shape=[jax.ShapeDtypeStruct((rank, user_width), F32)] * groups,
        in_specs=[SMEM] * 3 + [VMEM] + [ANY] * (2 + chips),
        out_specs=[VMEM] * groups,
        scratch_shapes=[
            pltpu.VMEM((slots, weeks, height, width), F32),
            pltpu.VMEM((slots, rank, width), F32),
            pltpu.VMEM((weeks, rank, width), F32),
            pltpu.VMEM((groups * user_width // height, rank, height), F32),
            pltpu.SemaphoreType.DMA((slots,)),
            pltpu.SemaphoreType.DMA((slots,)),
        ],
        compiler_params=pltpu.CompilerParams(vmem_limit_bytes=vmem_limit),
        name="mode1",
    )(counts, wanted_users, wanted_items, weeks_t, item_factor, sibling, *messages, tiles)
    m_users = parts[0]
    for step in range(1, groups):
        m_users = m_users + across_groups(parts[step], step)

    m_items = pl.pallas_call(
        functools.partial(collect_kernel, chips, slots, width),
        out_shape=jax.ShapeDtypeStruct(item_factor.shape, F32),
        in_specs=[SMEM] * rows + [ANY] * rows,
        out_specs=VMEM,
        scratch_shapes=[
            pltpu.VMEM((rows, slots, rank, width), F32),
            pltpu.SemaphoreType.DMA((rows, slots)),
        ],
        compiler_params=pltpu.CompilerParams(vmem_limit_bytes=vmem_limit),
        name="collect",
    )(*near, *far, *near_terms, *far_terms)
    return m_users, m_items


def solution(mesh):
    rows, groups = mesh.shape["users"], mesh.shape["items"]
    assert rows > 1 and rows & (rows - 1) == 0 and groups & (groups - 1) == 0
    return jax.shard_map(
        functools.partial(on_device, (rows, groups)),
        mesh=mesh,
        in_specs=(
            P("users", "items", None, None, None, None),
            P("users", "items", None),
            P("users", "items", None),
            P("users", "items"),
            P(None, ("users", "items")),
            P(None, ("items", "users")),
            P(),
        ),
        out_specs=(P(None, ("users", "items")), P(None, ("items", "users"))),
        check_vma=False,
    )
```

```python
import functools

import jax
import jax.numpy as jnp
from jax import lax
from jax.experimental import pallas as pl
from jax.experimental.pallas import tpu as pltpu
from jax.sharding import PartitionSpec as P

F32 = jnp.float32
BF16 = jnp.bfloat16
ANY = pl.BlockSpec(memory_space=pl.ANY)
HBM = pl.BlockSpec(memory_space=pltpu.HBM)
SMEM = pl.BlockSpec(memory_space=pltpu.SMEM)
VMEM = pl.BlockSpec(memory_space=pltpu.VMEM)


def columns(block, width):
    return pl.ds(pl.multiple_of(block * width, width), width)


def split(value):
    high = value.astype(BF16)
    return high, (value - high.astype(F32)).astype(BF16)


def serve_kernel(chips, slots, width, *refs):
    requests = refs[:chips]
    own, sibling = refs[chips : chips + 2]
    messages = refs[chips + 2 : 2 * chips + 1]
    near = refs[2 * chips + 1]
    me = lax.axis_index("users")
    per_device = own.shape[1] // width
    for step in range(1, chips):
        for slot in range(slots):
            index = requests[step][slot]
            device = index // per_device
            block = index % per_device
            for owner, source in ((me, own), (me ^ 1, sibling)):

                @pl.when(device == owner)
                def _():
                    messages[step - 1][:, slot * width : (slot + 1) * width] = source[
                        :, columns(block, width)
                    ]

    for step in range(chips):
        for slot in range(slots):
            near[step * slots + slot] = requests[step][slot]


def spread_weeks(weeks_t, spread):
    for week in range(spread.shape[0]):
        spread[week] = jnp.broadcast_to(weeks_t[:, week : week + 1], spread.shape[1:])


def prepare_kernel(count_ref, tiles, _, halves, held, sems):
    slots, weeks, height, width = tiles.shape
    count = count_ref[0, 0]

    def fetch(slot):
        return pltpu.make_async_copy(tiles.at[slot], held.at[slot], sems.at[slot])

    for slot in range(slots):

        @pl.when(slot < count)
        def _():
            fetch(slot).start()

    def work(slot, carry):
        fetch(slot).wait()

        def one(week, inner):
            high, low = split(held[slot, week])
            halves[slot, week, :, :width] = high
            halves[slot, week, :, width:] = low
            return inner

        return lax.fori_loop(0, weeks, one, carry, unroll=4)

    lax.fori_loop(0, count, work, 0)


def contract(spread, factor, tile, axis):
    rank, size = factor.shape[0], tile.shape[2] // 2
    total = jnp.zeros((2 * rank, 2 * size), F32)
    for week in range(0, tile.shape[0], 2):
        left, right = [], []
        for part in (week, week + 1):
            left.append(jnp.concatenate(split(spread[part] * factor), axis=0))
            if axis == 0:
                right.append(tile[part])
            else:
                right.append(
                    jnp.concatenate([tile[part, :, :size], tile[part, :, size:]], axis=0)
                )
        total += lax.dot_general(
            jnp.concatenate(left, axis=1),
            jnp.concatenate(right, axis=axis),
            (((1,), (axis,)), ((), ())),
            preferred_element_type=F32,
        )
    half = total[:rank] + total[rank:]
    return half[:, :size] + half[:, size:]


def mode2_kernel(groups, *refs):
    count_ref, blocks_ref, weeks_t = refs[:3]
    factors = refs[3 : 3 + groups]
    tiles, _, terms, spread = refs[3 + groups :]
    height, width = tiles.shape[2], tiles.shape[3] // 2
    me = lax.axis_index("items")
    count = count_ref[0, 0]
    per_device = factors[0].shape[1] // height
    spread_weeks(weeks_t, spread)
    terms[...] = jnp.zeros_like(terms)

    def work(slot, carry):
        block = blocks_ref[slot]
        source = (block // per_device) ^ me
        place = columns(block % per_device, height)
        users = factors[0][:, place]
        for step in range(1, groups):
            users = jnp.where(source == step, factors[step][:, place], users)
        terms[:, columns(slot, width)] = contract(spread, users, tiles.at[slot], 0)
        return carry

    lax.fori_loop(0, count, work, 0)


def mode1_kernel(groups, chips, *refs):
    count_ref, users_ref, items_ref, weeks_t, own, sibling = refs[:6]
    messages = refs[6 : 5 + chips]
    tiles = refs[5 + chips]
    parts = refs[6 + chips : 6 + chips + groups]
    spread, sums = refs[6 + chips + groups :]
    height, width = tiles.shape[2], tiles.shape[3] // 2
    me = lax.axis_index("users")
    column = lax.axis_index("items")
    count = count_ref[0, 0]
    per_device = own.shape[1] // width
    spread_weeks(weeks_t, spread)
    sums[...] = jnp.zeros_like(sums)

    def work(slot, carry):
        index = items_ref[slot]
        device = index // per_device
        place = columns(index % per_device, width)
        items = jnp.where(device == me, own[:, place], sibling[:, place])
        source = (device // 2) ^ (me // 2)
        for step in range(1, chips):
            items = jnp.where(source == step, messages[step - 1][:, columns(slot, width)], items)
        sums[users_ref[slot]] += contract(spread, items, tiles.at[slot], 1)
        return carry

    lax.fori_loop(0, count, work, 0)
    kept = parts[0].shape[1] // height
    for step in range(groups):
        first = (column ^ step) * kept
        for block in range(kept):
            parts[step][:, block * height : (block + 1) * height] = sums[first + block]


def collect_kernel(chips, slots, width, *refs):
    near, far = refs[:2]
    terms = refs[2 : 2 + 2 * chips]
    out = refs[2 + 2 * chips]
    per_device = out.shape[1] // width
    me = lax.axis_index("users")
    out[...] = jnp.zeros_like(out)
    for step in range(2 * chips):
        for slot in range(slots):
            index = (near, far)[step // chips][step % chips * slots + slot]

            @pl.when(index // per_device == me)
            def _():
                out[:, columns(index % per_device, width)] += terms[step][
                    :, slot * width : (slot + 1) * width
                ]


def on_device(sizes, tiles, user_blocks, item_blocks, counts, user_factor, item_factor, week_factor):
    rows, groups = sizes
    chips = rows // 2
    tiles = tiles[0, 0]
    slots, weeks, height, width = tiles.shape
    rank = week_factor.shape[1]
    wanted_users = user_blocks[0, 0]
    wanted_items = item_blocks[0, 0]
    weeks_t = week_factor.T
    params = pltpu.CompilerParams(vmem_limit_bytes=40 << 20)

    def across_chips(value, step):
        return lax.ppermute(value, "users", [(i, i ^ (2 * step)) for i in range(rows)])

    def across_cores(value):
        return lax.ppermute(value, "users", [(i, i ^ 1) for i in range(rows)])

    def across_groups(value, step):
        return lax.ppermute(value, "items", [(i, i ^ step) for i in range(groups)])

    requests = [wanted_items] + [across_chips(wanted_items, step) for step in range(1, chips)]
    sibling = across_cores(item_factor)
    row_factors = [user_factor] + [across_groups(user_factor, s) for s in range(1, groups)]

    block = jax.ShapeDtypeStruct((rank, slots * width), F32)
    *messages, near = pl.pallas_call(
        functools.partial(serve_kernel, chips, slots, width),
        out_shape=[block] * (chips - 1) + [jax.ShapeDtypeStruct((chips * slots,), jnp.int32)],
        in_specs=[SMEM] * chips + [VMEM] * 2,
        out_specs=[VMEM] * (chips - 1) + [SMEM],
        name="serve",
    )(*requests, item_factor, sibling)
    messages = [across_chips(m, step + 1) for step, m in enumerate(messages)]
    far = across_cores(near)

    halves = pl.pallas_call(
        prepare_kernel,
        out_shape=jax.ShapeDtypeStruct((slots, weeks, height, 2 * width), BF16),
        in_specs=[SMEM, HBM, ANY],
        out_specs=VMEM,
        scratch_shapes=[
            pltpu.VMEM((slots, weeks, height, width), F32),
            pltpu.SemaphoreType.DMA((slots,)),
        ],
        compiler_params=params,
        name="prepare",
    )(counts, tiles, near)

    user_width = user_factor.shape[1]
    parts = pl.pallas_call(
        functools.partial(mode1_kernel, groups, chips),
        out_shape=[jax.ShapeDtypeStruct((rank, user_width), F32)] * groups,
        in_specs=[SMEM] * 3 + [VMEM] * (3 + chips),
        out_specs=[VMEM] * groups,
        scratch_shapes=[
            pltpu.VMEM((weeks, rank, width), F32),
            pltpu.VMEM((groups * user_width // height, rank, height), F32),
        ],
        compiler_params=params,
        name="mode1",
    )(counts, wanted_users, wanted_items, weeks_t, item_factor, sibling, *messages, halves)

    terms = pl.pallas_call(
        functools.partial(mode2_kernel, groups),
        out_shape=block,
        in_specs=[SMEM] * 2 + [VMEM] * (2 + groups) + [ANY],
        out_specs=VMEM,
        scratch_shapes=[
            pltpu.VMEM((weeks, rank, height), F32),
        ],
        compiler_params=params,
        name="mode2",
    )(counts, wanted_users, weeks_t, *row_factors, halves, parts[0])
    near_terms = [terms] + [across_chips(terms, step) for step in range(1, chips)]
    far_terms = [across_cores(value) for value in near_terms]

    m_users = parts[0]
    for step in range(1, groups):
        m_users = m_users + across_groups(parts[step], step)

    m_items = pl.pallas_call(
        functools.partial(collect_kernel, chips, slots, width),
        out_shape=jax.ShapeDtypeStruct(item_factor.shape, F32),
        in_specs=[SMEM] * 2 + [VMEM] * rows,
        out_specs=VMEM,
        name="collect",
    )(near, far, *near_terms, *far_terms)
    return m_users, m_items


def solution(mesh):
    rows, groups = mesh.shape["users"], mesh.shape["items"]
    assert rows > 1 and rows & (rows - 1) == 0 and groups & (groups - 1) == 0
    return jax.shard_map(
        functools.partial(on_device, (rows, groups)),
        mesh=mesh,
        in_specs=(
            P("users", "items", None, None, None, None),
            P("users", "items", None),
            P("users", "items", None),
            P("users", "items"),
            P(None, ("users", "items")),
            P(None, ("items", "users")),
            P(),
        ),
        out_specs=(P(None, ("users", "items")), P(None, ("items", "users"))),
        check_vma=False,
    )
```

```python
import functools

import jax
import jax.numpy as jnp
from jax import lax
from jax.experimental import pallas as pl
from jax.experimental.pallas import tpu as pltpu
from jax.sharding import PartitionSpec as P

F32 = jnp.float32
BF16 = jnp.bfloat16
ANY = pl.BlockSpec(memory_space=pl.ANY)
HBM = pl.BlockSpec(memory_space=pltpu.HBM)
SMEM = pl.BlockSpec(memory_space=pltpu.SMEM)
VMEM = pl.BlockSpec(memory_space=pltpu.VMEM)


def columns(block, width):
    return pl.ds(pl.multiple_of(block * width, width), width)


def split(value):
    high = value.astype(BF16)
    return high, (value - high.astype(F32)).astype(BF16)


def prepare_kernel(*refs):
    count_ref, tiles, weeks_ref, user_factor, item_factor, users, items = refs[:7]
    halves, spread, own_users, own_items, users_out, items_out, held, sems = refs[7:]
    slots, weeks, height, width = tiles.shape
    count = count_ref[0, 0]

    def fetch(slot):
        return pltpu.make_async_copy(tiles.at[slot], held.at[slot], sems.at[slot])

    for slot in range(slots):

        @pl.when(slot < count)
        def _():
            fetch(slot).start()

    bring_users = pltpu.make_async_copy(user_factor, own_users, sems.at[slots])
    bring_items = pltpu.make_async_copy(item_factor, own_items, sems.at[slots + 1])
    bring_items.start()
    bring_users.start()
    users_out[...] = users[...]
    items_out[...] = items[...]
    weeks_t = weeks_ref[...].T
    for week in range(weeks):
        spread[week] = jnp.broadcast_to(weeks_t[:, week : week + 1], spread.shape[1:])

    def work(slot, carry):
        fetch(slot).wait()

        def one(week, inner):
            high, low = split(held[slot, week])
            halves[slot, week, :, :width] = high
            halves[slot, week, :, width:] = low
            return inner

        return lax.fori_loop(0, weeks, one, carry, unroll=8)

    lax.fori_loop(0, count, work, 0)
    bring_items.wait()
    bring_users.wait()


def serve_kernel(chips, width, *refs):
    requests = refs[:chips]
    own, sibling = refs[chips : chips + 2]
    messages = refs[chips + 2 : 2 * chips + 1]
    near = refs[2 * chips + 1]
    me = lax.axis_index("users")
    per_device = own.shape[1] // width
    asked = [request[...] for request in requests]
    for step in range(chips):
        near[step : step + 1, :] = asked[step]
    for step in range(1, chips):
        for slot in range(near.shape[1]):
            index = asked[step][0, slot]
            device = index // per_device
            block = index % per_device
            for owner, source in ((me, own), (me ^ 1, sibling)):

                @pl.when(device == owner)
                def _():
                    messages[step - 1][:, slot * width : (slot + 1) * width] = source[
                        :, columns(block, width)
                    ]


def contract(spread, factor, tile, axis):
    rank, size = factor.shape[0], tile.shape[2] // 2
    total = jnp.zeros((2 * rank, 2 * size), F32)
    for week in range(0, tile.shape[0], 2):
        left, right = [], []
        for part in (week, week + 1):
            left.append(jnp.concatenate(split(spread[part] * factor), axis=0))
            if axis == 0:
                right.append(tile[part])
            else:
                right.append(
                    jnp.concatenate([tile[part, :, :size], tile[part, :, size:]], axis=0)
                )
        total += lax.dot_general(
            jnp.concatenate(left, axis=1),
            jnp.concatenate(right, axis=axis),
            (((1,), (axis,)), ((), ())),
            preferred_element_type=F32,
        )
    half = total[:rank] + total[rank:]
    return half[:, :size] + half[:, size:]


def mode2_kernel(groups, *refs):
    count_ref, blocks_ref, spread = refs[:3]
    factors = refs[3 : 3 + groups]
    tiles, _, terms, picked = refs[3 + groups :]
    slots, _, height, width = tiles.shape
    width //= 2
    me = lax.axis_index("items")
    count = count_ref[0, 0]
    per_device = factors[0].shape[1] // height
    blocks = blocks_ref[...]
    for slot in range(slots):
        block = blocks[0, slot]
        source = (block // per_device) ^ me
        place = columns(block % per_device, height)
        users = factors[0][:, place]
        for step in range(1, groups):
            users = jnp.where(source == step, factors[step][:, place], users)
        picked[slot] = users
    terms[...] = jnp.zeros_like(terms)

    def work(slot, carry):
        terms[:, columns(slot, width)] = contract(spread, picked[slot], tiles.at[slot], 0)
        return carry

    lax.fori_loop(0, count, work, 0)


def mode1_kernel(groups, chips, *refs):
    count_ref, users_ref, items_ref, spread, own, sibling = refs[:6]
    messages = refs[6 : 5 + chips]
    tiles = refs[5 + chips]
    parts = refs[6 + chips : 6 + chips + groups]
    picked, terms, sums = refs[6 + chips + groups :]
    slots, _, height, width = tiles.shape
    width //= 2
    me = lax.axis_index("users")
    column = lax.axis_index("items")
    count = count_ref[0, 0]
    per_device = own.shape[1] // width
    wanted = items_ref[...]
    for slot in range(slots):
        index = wanted[0, slot]
        device = index // per_device
        place = columns(index % per_device, width)
        items = jnp.where(device == me, own[:, place], sibling[:, place])
        source = (device // 2) ^ (me // 2)
        for step in range(1, chips):
            here = messages[step - 1][:, slot * width : (slot + 1) * width]
            items = jnp.where(source == step, here, items)
        picked[slot] = items
    sums[...] = jnp.zeros_like(sums)

    def work(slot, carry):
        terms[slot] = contract(spread, picked[slot], tiles.at[slot], 1)
        return carry

    lax.fori_loop(0, count, work, 0)
    users = users_ref[...]
    for slot in range(slots):

        @pl.when(slot < count)
        def _():
            sums[users[0, slot]] += terms[slot]

    kept = parts[0].shape[1] // height
    for step in range(groups):
        first = (column ^ step) * kept
        for block in range(kept):
            parts[step][:, block * height : (block + 1) * height] = sums[first + block]


def collect_kernel(chips, width, *refs):
    near, far = refs[0][...], refs[1][...]
    terms = refs[2 : 2 + 2 * chips]
    out = refs[2 + 2 * chips]
    per_device = out.shape[1] // width
    me = lax.axis_index("users")
    out[...] = jnp.zeros_like(out)
    for step in range(2 * chips):
        for slot in range(near.shape[1]):
            index = (near, far)[step // chips][step % chips, slot]

            @pl.when(index // per_device == me)
            def _():
                out[:, columns(index % per_device, width)] += terms[step][
                    :, slot * width : (slot + 1) * width
                ]


def on_device(sizes, tiles, user_blocks, item_blocks, counts, user_factor, item_factor, week_factor):
    rows, groups = sizes
    chips = rows // 2
    tiles = tiles[0, 0]
    slots, weeks, height, width = tiles.shape
    rank = week_factor.shape[1]
    user_width = user_factor.shape[1]
    wanted_items = item_blocks[0]
    params = pltpu.CompilerParams(vmem_limit_bytes=40 << 20)
    product = pl.CostEstimate(
        flops=8 * slots * weeks * height * width * rank,
        bytes_accessed=8 * slots * weeks * height * width,
        transcendentals=0,
    )

    def across_chips(value, step):
        return lax.ppermute(value, "users", [(i, i ^ (2 * step)) for i in range(rows)])

    def across_cores(value):
        return lax.ppermute(value, "users", [(i, i ^ 1) for i in range(rows)])

    def across_groups(value, step):
        return lax.ppermute(value, "items", [(i, i ^ step) for i in range(groups)])

    def array(*shape, dtype=F32):
        return jax.ShapeDtypeStruct(shape, dtype)

    requests = [across_chips(wanted_items, step) for step in range(1, chips)]
    sibling = across_cores(item_factor)
    halves, spread, own_users, own_items, users_here, items_here = pl.pallas_call(
        prepare_kernel,
        out_shape=[
            array(slots, weeks, height, 2 * width, dtype=BF16),
            array(weeks, rank, height),
            array(rank, user_width),
            array(rank, item_factor.shape[1]),
            array(1, slots, dtype=jnp.int32),
            array(1, slots, dtype=jnp.int32),
        ],
        in_specs=[SMEM, HBM, VMEM, HBM, HBM, VMEM, VMEM],
        out_specs=[VMEM] * 6,
        scratch_shapes=[
            pltpu.VMEM((slots, weeks, height, width), F32),
            pltpu.SemaphoreType.DMA((slots + 2,)),
        ],
        compiler_params=params,
        cost_estimate=product,
        name="prepare",
    )(counts, tiles, week_factor, user_factor, item_factor, user_blocks[0], wanted_items)

    block = array(rank, slots * width)
    *messages, near = pl.pallas_call(
        functools.partial(serve_kernel, chips, width),
        out_shape=[block] * (chips - 1) + [array(chips, slots, dtype=jnp.int32)],
        in_specs=[VMEM] * (chips + 2),
        out_specs=[VMEM] * chips,
        name="serve",
    )(items_here, *requests, own_items, sibling)
    messages = [across_chips(m, step + 1) for step, m in enumerate(messages)]
    far = across_cores(near)
    row_factors = [own_users] + [across_groups(user_factor, s) for s in range(1, groups)]

    parts = pl.pallas_call(
        functools.partial(mode1_kernel, groups, chips),
        out_shape=[array(rank, user_width)] * groups,
        in_specs=[SMEM] + [VMEM] * (5 + chips),
        out_specs=[VMEM] * groups,
        scratch_shapes=[
            pltpu.VMEM((slots, rank, width), F32),
            pltpu.VMEM((slots, rank, height), F32),
            pltpu.VMEM((groups * user_width // height, rank, height), F32),
        ],
        compiler_params=params,
        cost_estimate=product,
        name="mode1",
    )(counts, users_here, items_here, spread, own_items, sibling, *messages, halves)

    terms = pl.pallas_call(
        functools.partial(mode2_kernel, groups),
        out_shape=block,
        in_specs=[SMEM] + [VMEM] * (3 + groups) + [ANY],
        out_specs=VMEM,
        scratch_shapes=[pltpu.VMEM((slots, rank, height), F32)],
        compiler_params=params,
        cost_estimate=product,
        name="mode2",
    )(counts, users_here, spread, *row_factors, halves, parts[0])
    near_terms = [terms] + [across_chips(terms, step) for step in range(1, chips)]
    far_terms = [across_cores(value) for value in near_terms]

    m_users = parts[0]
    for step in range(1, groups):
        m_users = m_users + across_groups(parts[step], step)

    m_items = pl.pallas_call(
        functools.partial(collect_kernel, chips, width),
        out_shape=array(*item_factor.shape),
        in_specs=[VMEM] * (2 + rows),
        out_specs=VMEM,
        name="collect",
    )(near, far, *near_terms, *far_terms)
    return m_users, m_items


def solution(mesh):
    rows, groups = mesh.shape["users"], mesh.shape["items"]
    assert rows > 1 and rows & (rows - 1) == 0 and groups & (groups - 1) == 0
    return jax.shard_map(
        functools.partial(on_device, (rows, groups)),
        mesh=mesh,
        in_specs=(
            P("users", "items", None, None, None, None),
            P("users", "items", None),
            P("users", "items", None),
            P("users", "items"),
            P(None, ("users", "items")),
            P(None, ("items", "users")),
            P(),
        ),
        out_specs=(P(None, ("users", "items")), P(None, ("items", "users"))),
        check_vma=False,
    )
```

```python
import functools

import jax
import jax.numpy as jnp
from jax import lax
from jax.experimental import pallas as pl
from jax.experimental.pallas import tpu as pltpu
from jax.sharding import PartitionSpec as P

F32 = jnp.float32
BF16 = jnp.bfloat16
ANY = pl.BlockSpec(memory_space=pl.ANY)
HBM = pl.BlockSpec(memory_space=pltpu.HBM)
SMEM = pl.BlockSpec(memory_space=pltpu.SMEM)
VMEM = pl.BlockSpec(memory_space=pltpu.VMEM)


def columns(block, width):
    return pl.ds(pl.multiple_of(block * width, width), width)


def split(value):
    high = value.astype(BF16)
    return high, (value - high.astype(F32)).astype(BF16)


def prepare_kernel(count_ref, tiles, weeks_ref, _, halves, spread, held, sems):
    slots, weeks, height, width = tiles.shape
    count = count_ref[0, 0]

    def fetch(slot):
        return pltpu.make_async_copy(tiles.at[slot], held.at[slot], sems.at[slot])

    for slot in range(slots):

        @pl.when(slot < count)
        def _():
            fetch(slot).start()

    weeks_t = weeks_ref[...].T
    for week in range(weeks):
        spread[week] = jnp.broadcast_to(weeks_t[:, week : week + 1], spread.shape[1:])

    def work(slot, carry):
        fetch(slot).wait()

        def one(week, inner):
            high, low = split(held[slot, week])
            halves[slot, week, :, :width] = high
            halves[slot, week, :, width:] = low
            return inner

        return lax.fori_loop(0, weeks, one, carry, unroll=8)

    lax.fori_loop(0, count, work, 0)


def serve_kernel(chips, width, requests, own, sibling, *messages):
    me = lax.axis_index("users")
    per_device = own.shape[1] // width
    for step in range(1, chips):
        for slot in range(requests.shape[1]):
            index = requests[(me // 2) ^ step, slot]
            device = index // per_device
            place = columns(index % per_device, width)
            for owner, source in ((me, own), (me ^ 1, sibling)):

                @pl.when(device == owner)
                def _():
                    messages[step - 1][:, slot * width : (slot + 1) * width] = source[:, place]


def contract(spread, factor, tile, axis):
    rank, size = factor.shape[0], tile.shape[2] // 2
    total = jnp.zeros((2 * rank, 2 * size), F32)
    for week in range(0, tile.shape[0], 2):
        left, right = [], []
        for part in (week, week + 1):
            left.append(jnp.concatenate(split(spread[part] * factor), axis=0))
            if axis == 0:
                right.append(tile[part])
            else:
                right.append(
                    jnp.concatenate([tile[part, :, :size], tile[part, :, size:]], axis=0)
                )
        total += lax.dot_general(
            jnp.concatenate(left, axis=1),
            jnp.concatenate(right, axis=axis),
            (((1,), (axis,)), ((), ())),
            preferred_element_type=F32,
        )
    half = total[:rank] + total[rank:]
    return half[:, :size] + half[:, size:]


def modes_kernel(groups, chips, *refs):
    count_ref, users_ref, items_ref, spread = refs[:4]
    factors = refs[4 : 4 + groups]
    own, sibling = refs[4 + groups : 6 + groups]
    messages = refs[6 + groups : 5 + groups + chips]
    tiles = refs[5 + groups + chips]
    parts = refs[6 + groups + chips : 6 + 2 * groups + chips]
    terms, sums = refs[6 + 2 * groups + chips :]
    slots, _, height, width = tiles.shape
    width //= 2
    me = lax.axis_index("users")
    column = lax.axis_index("items")
    count = count_ref[0, 0]
    kept = factors[0].shape[1] // height
    per_device = own.shape[1] // width
    sums[...] = jnp.zeros_like(sums)
    terms[...] = jnp.zeros_like(terms)

    def work(slot, carry):
        block = users_ref[0, slot]
        source = (block // kept) ^ column
        place = columns(block % kept, height)
        users = factors[0][:, place]
        for step in range(1, groups):
            users = jnp.where(source == step, factors[step][:, place], users)
        index = items_ref[0, slot]
        device = index // per_device
        place = columns(index % per_device, width)
        items = jnp.where(device == me, own[:, place], sibling[:, place])
        source = (device // 2) ^ (me // 2)
        here = columns(slot, width)
        for step in range(1, chips):
            items = jnp.where(source == step, messages[step - 1][:, here], items)
        sums[block] += contract(spread, items, tiles.at[slot], 1)
        term = contract(spread, users, tiles.at[slot], 0)
        for chip in range(chips):
            terms[chip, :, here] = term
        return carry

    lax.fori_loop(0, count, work, 0)
    for step in range(groups):
        first = (column ^ step) * kept
        for block in range(kept):
            parts[step][:, block * height : (block + 1) * height] = sums[first + block]


def collect_kernel(groups, ids, terms, *refs):
    parts = refs[:groups]
    m_users, own, other = refs[groups:]
    chips, slots = ids.shape
    width = terms.shape[2] // slots
    per_device = own.shape[1] // width
    me = lax.axis_index("users")
    own[...] = jnp.zeros_like(own)
    other[...] = jnp.zeros_like(other)
    for chip in range(chips):
        for slot in range(slots):
            index = ids[chip, slot]
            device = index // per_device
            place = columns(index % per_device, width)
            for owner, target in ((me, own), (me ^ 1, other)):

                @pl.when(device == owner)
                def _():
                    target[:, place] += terms[chip, :, slot * width : (slot + 1) * width]

    total = parts[0][...]
    for part in parts[1:]:
        total += part[...]
    m_users[...] = total


def on_device(sizes, tiles, user_blocks, item_blocks, counts, user_factor, item_factor, week_factor):
    rows, groups = sizes
    chips = rows // 2
    tiles = tiles[0, 0]
    slots, weeks, height, width = tiles.shape
    rank = week_factor.shape[1]
    user_width = user_factor.shape[1]

    def limit(mebibytes):
        return pltpu.CompilerParams(vmem_limit_bytes=mebibytes << 20)

    def swap_chips(value):
        same_core = [list(range(core, rows, 2)) for core in range(2)]
        return lax.all_to_all(value, "users", 0, 0, axis_index_groups=same_core, tiled=True)

    def across_chips(value, step):
        return lax.ppermute(value, "users", [(i, i ^ (2 * step)) for i in range(rows)])

    def across_cores(value):
        return lax.ppermute(value, "users", [(i, i ^ 1) for i in range(rows)])

    def across_groups(value, step):
        return lax.ppermute(value, "items", [(i, i ^ step) for i in range(groups)])

    def array(*shape, dtype=F32):
        return jax.ShapeDtypeStruct(shape, dtype)

    sibling = across_cores(item_factor)
    near = swap_chips(jnp.broadcast_to(item_blocks[0], (chips, slots)))
    row_factors = [user_factor] + [across_groups(user_factor, s) for s in range(1, groups)]

    served = pl.pallas_call(
        functools.partial(serve_kernel, chips, width),
        out_shape=[array(rank, slots * width)] * (chips - 1),
        in_specs=[SMEM] + [VMEM] * 2,
        out_specs=[VMEM] * (chips - 1),
        compiler_params=limit(4),
        name="serve",
    )(near, item_factor, sibling)
    messages = [across_chips(value, step + 1) for step, value in enumerate(served)]

    halves, spread = pl.pallas_call(
        prepare_kernel,
        out_shape=[
            array(slots, weeks, height, 2 * width, dtype=BF16),
            array(weeks, rank, height),
        ],
        in_specs=[SMEM, HBM, VMEM, ANY],
        out_specs=[VMEM] * 2,
        scratch_shapes=[
            pltpu.VMEM((slots, weeks, height, width), F32),
            pltpu.SemaphoreType.DMA((slots,)),
        ],
        compiler_params=limit(40),
        name="prepare",
    )(counts, tiles, week_factor, served[0])

    *parts, terms = pl.pallas_call(
        functools.partial(modes_kernel, groups, chips),
        out_shape=[array(rank, user_width)] * groups + [array(chips, rank, slots * width)],
        in_specs=[SMEM] * 3 + [VMEM] * (3 + groups + chips - 1 + 1),
        out_specs=[VMEM] * (groups + 1),
        scratch_shapes=[pltpu.VMEM((groups * user_width // height, rank, height), F32)],
        compiler_params=limit(8),
        name="modes",
    )(
        counts,
        user_blocks[0],
        item_blocks[0],
        spread,
        *row_factors,
        item_factor,
        sibling,
        *messages,
        halves,
    )
    arrived = [parts[0]] + [across_groups(parts[step], step) for step in range(1, groups)]
    m_users, own, other = pl.pallas_call(
        functools.partial(collect_kernel, groups),
        out_shape=[array(rank, user_width)] + [array(*item_factor.shape)] * 2,
        in_specs=[SMEM] + [VMEM] * (1 + groups),
        out_specs=[VMEM] * 3,
        compiler_params=limit(4),
        name="collect",
    )(near, swap_chips(terms), *arrived)
    m_items = own + across_cores(other)
    return m_users, m_items


def solution(mesh):
    rows, groups = mesh.shape["users"], mesh.shape["items"]
    assert rows > 1 and rows & (rows - 1) == 0 and groups & (groups - 1) == 0
    return jax.shard_map(
        functools.partial(on_device, (rows, groups)),
        mesh=mesh,
        in_specs=(
            P("users", "items", None, None, None, None),
            P("users", "items", None),
            P("users", "items", None),
            P("users", "items"),
            P(None, ("users", "items")),
            P(None, ("items", "users")),
            P(),
        ),
        out_specs=(P(None, ("users", "items")), P(None, ("items", "users"))),
        check_vma=False,
    )
```

```python
import functools

import jax
import jax.numpy as jnp
from jax import lax
from jax.experimental import pallas as pl
from jax.experimental.pallas import tpu as pltpu
from jax.sharding import PartitionSpec as P

F32 = jnp.float32
BF16 = jnp.bfloat16
ANY = pl.BlockSpec(memory_space=pl.ANY)
HBM = pl.BlockSpec(memory_space=pltpu.HBM)
SMEM = pl.BlockSpec(memory_space=pltpu.SMEM)
VMEM = pl.BlockSpec(memory_space=pltpu.VMEM)


def columns(block, width):
    return pl.ds(pl.multiple_of(block * width, width), width)


def split(value):
    high = value.astype(BF16)
    return high, (value - high.astype(F32)).astype(BF16)


def prepare_kernel(count_ref, tiles, weeks_ref, _, halves, spread, doubled, held, sems):
    slots, weeks, height, width = tiles.shape
    count = count_ref[0, 0]

    def fetch(slot):
        return pltpu.make_async_copy(tiles.at[slot], held.at[slot], sems.at[slot])

    for slot in range(slots):

        @pl.when(slot < count)
        def _():
            fetch(slot).start()

    doubled[...] = jnp.concatenate([weeks_ref[...]] * 2, axis=1)
    weeks_t = weeks_ref[...].T
    for week in range(weeks):
        spread[week] = jnp.broadcast_to(weeks_t[:, week : week + 1], spread.shape[1:])

    def work(slot, carry):
        fetch(slot).wait()

        def one(week, inner):
            high, low = split(held[slot, week])
            halves[slot, week, :, :width] = high
            halves[slot, week, :, width:] = low
            return inner

        return lax.fori_loop(0, weeks, one, carry, unroll=8)

    lax.fori_loop(0, count, work, 0)


def serve_kernel(chips, width, requests, own, sibling, *messages):
    me = lax.axis_index("users")
    per_device = own.shape[1] // width
    for step in range(1, chips):
        for slot in range(requests.shape[1]):
            index = requests[step, slot]
            device = index // per_device
            place = columns(index % per_device, width)
            for owner, source in ((me, own), (me ^ 1, sibling)):

                @pl.when(device == owner)
                def _():
                    messages[step - 1][:, slot * width : (slot + 1) * width] = source[:, place]


def user_term(doubled, items, tile):
    weeks, height, width = tile.shape
    width //= 2
    rank = items.shape[0]
    factor = jnp.concatenate([items, items], axis=0).T
    is_high = lax.broadcasted_iota(jnp.int32, factor.shape, 1) < rank
    total = jnp.zeros((2 * height, 2 * rank), F32)
    for week in range(0, weeks, 2):
        left, right = [], []
        for part in (week, week + 1):
            left.append(jnp.concatenate([tile[part, :, :width], tile[part, :, width:]], axis=0))
            product = factor * doubled[part : part + 1, :]
            rest = product - product.astype(BF16).astype(F32)
            right.append(jnp.where(is_high, product, rest).astype(BF16))
        total += jnp.dot(
            jnp.concatenate(left, axis=1),
            jnp.concatenate(right, axis=0),
            preferred_element_type=F32,
        )
    half = (total[:height] + total[height:]).T
    return half[:rank] + half[rank:]


def item_term(spread, users, tile):
    weeks, height, width = tile.shape
    width //= 2
    rank = users.shape[0]
    total = jnp.zeros((2 * rank, 2 * width), F32)
    for week in range(0, weeks, 2):
        left = [
            jnp.concatenate(split(spread[part] * users), axis=0) for part in (week, week + 1)
        ]
        total += jnp.dot(
            jnp.concatenate(left, axis=1),
            jnp.concatenate([tile[week], tile[week + 1]], axis=0),
            preferred_element_type=F32,
        )
    half = total[:rank] + total[rank:]
    return half[:, :width] + half[:, width:]


def modes_kernel(groups, chips, *refs):
    count_ref, users_ref, items_ref, spread, doubled, tiles, own, sibling = refs[:8]
    factors = refs[8 : 8 + groups]
    messages = refs[8 + groups : 7 + groups + chips]
    parts = refs[7 + groups + chips : 7 + 2 * groups + chips]
    terms, sums = refs[7 + 2 * groups + chips :]
    slots, _, height, width = tiles.shape
    width //= 2
    me = lax.axis_index("users")
    column = lax.axis_index("items")
    count = count_ref[0, 0]
    kept = factors[0].shape[1] // height
    per_device = own.shape[1] // width
    sums[...] = jnp.zeros_like(sums)
    terms[...] = jnp.zeros_like(terms)

    def work(slot, carry):
        block = users_ref[0, slot]
        source = (block // kept) ^ column
        place = columns(block % kept, height)
        users = factors[0][:, place]
        for step in range(1, groups):
            users = jnp.where(source == step, factors[step][:, place], users)
        index = items_ref[0, slot]
        device = index // per_device
        place = columns(index % per_device, width)
        items = jnp.where(device == me, own[:, place], sibling[:, place])
        source = (device // 2) ^ (me // 2)
        here = columns(slot, width)
        for step in range(1, chips):
            items = jnp.where(source == step, messages[step - 1][:, here], items)
        sums[block] += user_term(doubled, items, tiles.at[slot])
        terms[:, here] = item_term(spread, users, tiles.at[slot])
        return carry

    lax.fori_loop(0, count, work, 0)
    for step in range(groups):
        first = (column ^ step) * kept
        for block in range(kept):
            parts[step][:, block * height : (block + 1) * height] = sums[first + block]


def collect_kernel(ids, *refs):
    *terms, own, other = refs
    slots = ids.shape[1]
    width = terms[0].shape[1] // slots
    per_device = own.shape[1] // width
    me = lax.axis_index("users")
    own[...] = jnp.zeros_like(own)
    other[...] = jnp.zeros_like(other)
    for step, term in enumerate(terms):
        for slot in range(slots):
            index = ids[step, slot]
            device = index // per_device
            place = columns(index % per_device, width)
            for owner, target in ((me, own), (me ^ 1, other)):

                @pl.when(device == owner)
                def _():
                    target[:, place] += term[:, slot * width : (slot + 1) * width]


def on_device(sizes, tiles, user_blocks, item_blocks, counts, user_factor, item_factor, week_factor):
    rows, groups = sizes
    chips = rows // 2
    tiles = tiles[0, 0]
    slots, weeks, height, width = tiles.shape
    rank = week_factor.shape[1]
    user_width = user_factor.shape[1]

    def limit(mebibytes):
        return pltpu.CompilerParams(vmem_limit_bytes=mebibytes << 20)

    def across_chips(value, step):
        return lax.ppermute(value, "users", [(i, i ^ (2 * step)) for i in range(rows)])

    def across_cores(value):
        return lax.ppermute(value, "users", [(i, i ^ 1) for i in range(rows)])

    def across_groups(value, step):
        return lax.ppermute(value, "items", [(i, i ^ step) for i in range(groups)])

    def array(*shape, dtype=F32):
        return jax.ShapeDtypeStruct(shape, dtype)

    sibling = across_cores(item_factor)
    asked = [item_blocks[0]] + [across_chips(item_blocks[0], step) for step in range(1, chips)]
    near = jnp.concatenate(asked, axis=0)
    row_factors = [user_factor] + [across_groups(user_factor, s) for s in range(1, groups)]

    served = pl.pallas_call(
        functools.partial(serve_kernel, chips, width),
        out_shape=[array(rank, slots * width)] * (chips - 1),
        in_specs=[SMEM] + [VMEM] * 2,
        out_specs=[VMEM] * (chips - 1),
        compiler_params=limit(4),
        name="serve",
    )(near, item_factor, sibling)
    messages = [across_chips(value, step + 1) for step, value in enumerate(served)]

    halves, spread, doubled = pl.pallas_call(
        prepare_kernel,
        out_shape=[
            array(slots, weeks, height, 2 * width, dtype=BF16),
            array(weeks, rank, height),
            array(weeks, 2 * rank),
        ],
        in_specs=[SMEM, HBM, VMEM, ANY],
        out_specs=[VMEM] * 3,
        scratch_shapes=[
            pltpu.VMEM((slots, weeks, height, width), F32),
            pltpu.SemaphoreType.DMA((slots,)),
        ],
        compiler_params=limit(40),
        name="prepare",
    )(counts, tiles, week_factor, served[0])

    *parts, terms = pl.pallas_call(
        functools.partial(modes_kernel, groups, chips),
        out_shape=[array(rank, user_width)] * groups + [array(rank, slots * width)],
        in_specs=[SMEM] * 3 + [VMEM] * (4 + groups + chips),
        out_specs=[VMEM] * (groups + 1),
        scratch_shapes=[pltpu.VMEM((groups * user_width // height, rank, height), F32)],
        compiler_params=limit(8),
        name="modes",
    )(
        counts,
        user_blocks[0],
        item_blocks[0],
        spread,
        doubled,
        halves,
        item_factor,
        sibling,
        *row_factors,
        *messages,
    )
    near_terms = [terms] + [across_chips(terms, step) for step in range(1, chips)]
    own, other = pl.pallas_call(
        collect_kernel,
        out_shape=[array(*item_factor.shape)] * 2,
        in_specs=[SMEM] + [VMEM] * chips,
        out_specs=[VMEM] * 2,
        compiler_params=limit(4),
        name="collect",
    )(near, *near_terms)
    m_items = own + across_cores(other)

    m_users = parts[0]
    for step in range(1, groups):
        m_users = m_users + across_groups(parts[step], step)
    return m_users, m_items


def solution(mesh):
    rows, groups = mesh.shape["users"], mesh.shape["items"]
    assert rows > 1 and rows & (rows - 1) == 0 and groups & (groups - 1) == 0
    return jax.shard_map(
        functools.partial(on_device, (rows, groups)),
        mesh=mesh,
        in_specs=(
            P("users", "items", None, None, None, None),
            P("users", "items", None),
            P("users", "items", None),
            P("users", "items"),
            P(None, ("users", "items")),
            P(None, ("items", "users")),
            P(),
        ),
        out_specs=(P(None, ("users", "items")), P(None, ("items", "users"))),
        check_vma=False,
    )
```

```python
import functools

import jax
import jax.numpy as jnp
from jax import lax
from jax.experimental import pallas as pl
from jax.experimental.pallas import tpu as pltpu
from jax.sharding import PartitionSpec as P

F32 = jnp.float32
BF16 = jnp.bfloat16
ANY = pl.BlockSpec(memory_space=pl.ANY)
HBM = pl.BlockSpec(memory_space=pltpu.HBM)
SMEM = pl.BlockSpec(memory_space=pltpu.SMEM)
VMEM = pl.BlockSpec(memory_space=pltpu.VMEM)


def columns(block, width):
    return pl.ds(pl.multiple_of(block * width, width), width)


def split(value):
    high = value.astype(BF16)
    return high, (value - high.astype(F32)).astype(BF16)


def prepare_kernel(count_ref, tiles, weeks_ref, _, halves, spread, held, sems):
    slots, weeks, height, width = tiles.shape
    count = count_ref[0, 0]

    def fetch(slot):
        return pltpu.make_async_copy(tiles.at[slot], held.at[slot], sems.at[slot])

    for slot in range(slots):

        @pl.when(slot < count)
        def _():
            fetch(slot).start()

    weeks_t = weeks_ref[...].T
    for week in range(weeks):
        spread[week] = jnp.broadcast_to(weeks_t[:, week : week + 1], spread.shape[1:])

    def work(slot, carry):
        fetch(slot).wait()

        def one(week, inner):
            high, low = split(held[slot, week])
            halves[slot, week, :, :width] = high
            halves[slot, week, :, width:] = low
            return inner

        return lax.fori_loop(0, weeks, one, carry, unroll=8)

    lax.fori_loop(0, count, work, 0)


def serve_kernel(chips, width, requests, own, sibling, *messages):
    me = lax.axis_index("users")
    per_device = own.shape[1] // width
    for step in range(1, chips):
        for slot in range(requests.shape[1]):
            index = requests[step, slot]
            device = index // per_device
            place = columns(index % per_device, width)
            for owner, source in ((me, own), (me ^ 1, sibling)):

                @pl.when(device == owner)
                def _():
                    messages[step - 1][:, slot * width : (slot + 1) * width] = source[:, place]


def user_term(spread, items, tile):
    weeks, height, width = tile.shape
    width //= 2
    rank = items.shape[0]
    total = jnp.zeros((2 * rank, 2 * height), F32)
    for week in range(0, weeks, 2):
        left, right = [], []
        for part in (week, week + 1):
            left.append(jnp.concatenate(split(spread[part] * items), axis=0))
            right.append(jnp.concatenate([tile[part, :, :width], tile[part, :, width:]], axis=0))
        total += lax.dot_general(
            jnp.concatenate(left, axis=1),
            jnp.concatenate(right, axis=1),
            (((1,), (1,)), ((), ())),
            preferred_element_type=F32,
        )
    half = total[:rank] + total[rank:]
    return half[:, :height] + half[:, height:]


def item_term(spread, users, tile):
    weeks, height, width = tile.shape
    width //= 2
    rank = users.shape[0]
    total = jnp.zeros((2 * rank, 2 * width), F32)
    for week in range(0, weeks, 2):
        left = [
            jnp.concatenate(split(spread[part] * users), axis=0) for part in (week, week + 1)
        ]
        total += jnp.dot(
            jnp.concatenate(left, axis=1),
            jnp.concatenate([tile[week], tile[week + 1]], axis=0),
            preferred_element_type=F32,
        )
    half = total[:rank] + total[rank:]
    return half[:, :width] + half[:, width:]


def modes_kernel(groups, chips, *refs):
    count_ref, users_ref, items_ref, spread, tiles, own, sibling = refs[:7]
    factors = refs[7 : 7 + groups]
    messages = refs[7 + groups : 6 + groups + chips]
    even, odd, terms, sums = refs[6 + groups + chips :]
    slots, _, height, width = tiles.shape
    width //= 2
    me = lax.axis_index("users")
    column = lax.axis_index("items")
    count = count_ref[0, 0]
    kept = factors[0].shape[1] // height
    per_device = own.shape[1] // width
    sums[...] = jnp.zeros_like(sums)
    terms[...] = jnp.zeros_like(terms)

    def work(slot, carry):
        block = users_ref[0, slot]
        source = (block // kept) ^ column
        place = columns(block % kept, height)
        users = factors[0][:, place]
        for step in range(1, groups):
            users = jnp.where(source == step, factors[step][:, place], users)
        index = items_ref[0, slot]
        device = index // per_device
        place = columns(index % per_device, width)
        items = jnp.where(device == me, own[:, place], sibling[:, place])
        source = (device // 2) ^ (me // 2)
        here = columns(slot, width)
        for step in range(1, chips):
            items = jnp.where(source == step, messages[step - 1][:, here], items)
        sums[block] += user_term(spread, items, tiles.at[slot])
        terms[:, here] = item_term(spread, users, tiles.at[slot])
        return carry

    lax.fori_loop(0, count, work, 0)
    for step in range(groups):
        first = (column ^ step) * kept
        for block in range(kept):
            target = (even, odd)[step % 2]
            target[step // 2, :, block * height : (block + 1) * height] = sums[first + block]


def collect_kernel(ids, *refs):
    *terms, own, other = refs
    slots = ids.shape[1]
    width = terms[0].shape[1] // slots
    per_device = own.shape[1] // width
    me = lax.axis_index("users")
    own[...] = jnp.zeros_like(own)
    other[...] = jnp.zeros_like(other)
    for step, term in enumerate(terms):
        for slot in range(slots):
            index = ids[step, slot]
            device = index // per_device
            place = columns(index % per_device, width)
            for owner, target in ((me, own), (me ^ 1, other)):

                @pl.when(device == owner)
                def _():
                    target[:, place] += term[:, slot * width : (slot + 1) * width]


def on_device(sizes, tiles, user_blocks, item_blocks, counts, user_factor, item_factor, week_factor):
    rows, groups = sizes
    chips = rows // 2
    tiles = tiles[0, 0]
    slots, weeks, height, width = tiles.shape
    rank = week_factor.shape[1]
    user_width = user_factor.shape[1]

    def limit(mebibytes):
        return pltpu.CompilerParams(vmem_limit_bytes=mebibytes << 20)

    def across_chips(value, step):
        return lax.ppermute(value, "users", [(i, i ^ (2 * step)) for i in range(rows)])

    def across_cores(value):
        return lax.ppermute(value, "users", [(i, i ^ 1) for i in range(rows)])

    def across_groups(value, step):
        return lax.ppermute(value, "items", [(i, i ^ step) for i in range(groups)])

    def array(*shape, dtype=F32):
        return jax.ShapeDtypeStruct(shape, dtype)

    sibling = across_cores(item_factor)
    asked = [item_blocks[0]] + [across_chips(item_blocks[0], step) for step in range(1, chips)]
    near = jnp.concatenate(asked, axis=0)
    row_factors = {0: user_factor}
    step = groups // 2
    while step:
        row_factors |= {at ^ step: across_groups(v, step) for at, v in row_factors.items()}
        step //= 2

    served = pl.pallas_call(
        functools.partial(serve_kernel, chips, width),
        out_shape=[array(rank, slots * width)] * (chips - 1),
        in_specs=[SMEM] + [VMEM] * 2,
        out_specs=[VMEM] * (chips - 1),
        compiler_params=limit(4),
        name="serve",
    )(near, item_factor, sibling)
    messages = [across_chips(value, step + 1) for step, value in enumerate(served)]

    halves, spread = pl.pallas_call(
        prepare_kernel,
        out_shape=[
            array(slots, weeks, height, 2 * width, dtype=BF16),
            array(weeks, rank, height),
        ],
        in_specs=[SMEM, HBM, VMEM, ANY],
        out_specs=[VMEM] * 2,
        scratch_shapes=[
            pltpu.VMEM((slots, weeks, height, width), F32),
            pltpu.SemaphoreType.DMA((slots,)),
        ],
        compiler_params=limit(40),
        name="prepare",
    )(counts, tiles, week_factor, served[0])

    even, odd, terms = pl.pallas_call(
        functools.partial(modes_kernel, groups, chips),
        out_shape=[array(groups // 2, rank, user_width)] * 2 + [array(rank, slots * width)],
        in_specs=[SMEM] * 3 + [VMEM] * (3 + groups + chips),
        out_specs=[VMEM] * 3,
        scratch_shapes=[pltpu.VMEM((groups * user_width // height, rank, height), F32)],
        compiler_params=limit(8),
        name="modes",
    )(
        counts,
        user_blocks[0],
        item_blocks[0],
        spread,
        halves,
        item_factor,
        sibling,
        *(row_factors[step] for step in range(groups)),
        *messages,
    )
    near_terms = [terms] + [across_chips(terms, step) for step in range(1, chips)]
    own, other = pl.pallas_call(
        collect_kernel,
        out_shape=[array(*item_factor.shape)] * 2,
        in_specs=[SMEM] + [VMEM] * chips,
        out_specs=[VMEM] * 2,
        compiler_params=limit(4),
        name="collect",
    )(near, *near_terms)
    m_items = own + across_cores(other)

    kept, sent, step = even, odd, 1
    while step < groups:
        arrived = across_groups(sent, step)
        kept, sent = kept[0::2] + arrived[0::2], kept[1::2] + arrived[1::2]
        step *= 2
    m_users = kept[0]
    return m_users, m_items


def solution(mesh):
    rows, groups = mesh.shape["users"], mesh.shape["items"]
    assert rows > 1 and rows & (rows - 1) == 0 and groups > 1 and groups & (groups - 1) == 0
    return jax.shard_map(
        functools.partial(on_device, (rows, groups)),
        mesh=mesh,
        in_specs=(
            P("users", "items", None, None, None, None),
            P("users", "items", None),
            P("users", "items", None),
            P("users", "items"),
            P(None, ("users", "items")),
            P(None, ("items", "users")),
            P(),
        ),
        out_specs=(P(None, ("users", "items")), P(None, ("items", "users"))),
        check_vma=False,
    )
```

```python
import functools

import jax
import jax.numpy as jnp
from jax import lax
from jax.experimental import pallas as pl
from jax.experimental.pallas import tpu as pltpu
from jax.sharding import PartitionSpec as P

F32 = jnp.float32
BF16 = jnp.bfloat16
ANY = pl.BlockSpec(memory_space=pl.ANY)
HBM = pl.BlockSpec(memory_space=pltpu.HBM)
SMEM = pl.BlockSpec(memory_space=pltpu.SMEM)
VMEM = pl.BlockSpec(memory_space=pltpu.VMEM)


def columns(block, width):
    return pl.ds(pl.multiple_of(block * width, width), width)


def split(value):
    high = value.astype(BF16)
    return high, (value - high.astype(F32)).astype(BF16)


def prepare_kernel(count_ref, tiles, weeks_ref, _, halves, spread, held, sems):
    slots, weeks, height, width = tiles.shape
    count = count_ref[0, 0]

    def fetch(slot):
        return pltpu.make_async_copy(tiles.at[slot], held.at[slot], sems.at[slot])

    for slot in range(slots):

        @pl.when(slot < count)
        def _():
            fetch(slot).start()

    weeks_t = weeks_ref[...].T
    for week in range(weeks):
        spread[week] = jnp.broadcast_to(weeks_t[:, week : week + 1], spread.shape[1:])

    def work(slot, carry):
        fetch(slot).wait()

        def one(week, inner):
            high, low = split(held[slot, week])
            halves[slot, week, :, :width] = high
            halves[slot, week, :, width:] = low
            return inner

        return lax.fori_loop(0, weeks, one, carry, unroll=8)

    lax.fori_loop(0, count, work, 0)


def serve_kernel(chips, width, requests, own, sibling, users, *refs):
    *messages, users_out = refs
    users_out[...] = users[...]
    me = lax.axis_index("users")
    per_device = own.shape[1] // width
    for step in range(1, chips):
        for slot in range(requests.shape[1]):
            index = requests[step, slot]
            device = index // per_device
            place = columns(index % per_device, width)
            for owner, source in ((me, own), (me ^ 1, sibling)):

                @pl.when(device == owner)
                def _():
                    messages[step - 1][:, slot * width : (slot + 1) * width] = source[:, place]


def user_term(spread, items, tile):
    weeks, height, width = tile.shape
    width //= 2
    rank = items.shape[0]
    total = jnp.zeros((2 * rank, 2 * height), F32)
    for week in range(0, weeks, 2):
        left, right = [], []
        for part in (week, week + 1):
            left.append(jnp.concatenate(split(spread[part] * items), axis=0))
            right.append(jnp.concatenate([tile[part, :, :width], tile[part, :, width:]], axis=0))
        total += lax.dot_general(
            jnp.concatenate(left, axis=1),
            jnp.concatenate(right, axis=1),
            (((1,), (1,)), ((), ())),
            preferred_element_type=F32,
        )
    half = total[:rank] + total[rank:]
    return half[:, :height] + half[:, height:]


def item_term(spread, users, tile):
    weeks, height, width = tile.shape
    width //= 2
    rank = users.shape[0]
    total = jnp.zeros((2 * rank, 2 * width), F32)
    for week in range(0, weeks, 2):
        left = [
            jnp.concatenate(split(spread[part] * users), axis=0) for part in (week, week + 1)
        ]
        total += jnp.dot(
            jnp.concatenate(left, axis=1),
            jnp.concatenate([tile[week], tile[week + 1]], axis=0),
            preferred_element_type=F32,
        )
    half = total[:rank] + total[rank:]
    return half[:, :width] + half[:, width:]


def mode1_kernel(groups, count_ref, users_ref, items_ref, spread, tiles, own, sibling, *refs):
    messages, (even, odd, sums) = refs[: -2 - groups], refs[-3:]
    height, width = tiles.shape[2], tiles.shape[3] // 2
    me = lax.axis_index("users")
    column = lax.axis_index("items")
    per_device = own.shape[1] // width
    kept = even.shape[2] // height
    sums[...] = jnp.zeros_like(sums)

    def work(slot, carry):
        index = items_ref[0, slot]
        device = index // per_device
        place = columns(index % per_device, width)
        items = jnp.where(device == me, own[:, place], sibling[:, place])
        source = (device // 2) ^ (me // 2)
        here = columns(slot, width)
        for step, message in enumerate(messages):
            items = jnp.where(source == step + 1, message[:, here], items)
        sums[users_ref[0, slot]] += user_term(spread, items, tiles.at[slot])
        return carry

    lax.fori_loop(0, count_ref[0, 0], work, 0)
    for step in range(groups):
        first = (column ^ step) * kept
        for block in range(kept):
            target = (even, odd)[step % 2]
            target[step // 2, :, block * height : (block + 1) * height] = sums[first + block]


def mode2_kernel(count_ref, users_ref, spread, tiles, _, *refs):
    *factors, terms = refs
    height, width = tiles.shape[2], tiles.shape[3] // 2
    column = lax.axis_index("items")
    kept = factors[0].shape[1] // height
    terms[...] = jnp.zeros_like(terms)

    def work(slot, carry):
        block = users_ref[0, slot]
        source = (block // kept) ^ column
        place = columns(block % kept, height)
        users = factors[0][:, place]
        for step in range(1, len(factors)):
            users = jnp.where(source == step, factors[step][:, place], users)
        terms[:, columns(slot, width)] = item_term(spread, users, tiles.at[slot])
        return carry

    lax.fori_loop(0, count_ref[0, 0], work, 0)


def collect_kernel(ids, *refs):
    *terms, own, other = refs
    slots = ids.shape[1]
    width = terms[0].shape[1] // slots
    per_device = own.shape[1] // width
    me = lax.axis_index("users")
    own[...] = jnp.zeros_like(own)
    other[...] = jnp.zeros_like(other)
    for step, term in enumerate(terms):
        for slot in range(slots):
            index = ids[step, slot]
            device = index // per_device
            place = columns(index % per_device, width)
            for owner, target in ((me, own), (me ^ 1, other)):

                @pl.when(device == owner)
                def _():
                    target[:, place] += term[:, slot * width : (slot + 1) * width]


def finish_users_kernel(kept, arrived, total, done):
    total[...] = kept[...] + arrived[...]
    done[...] = jnp.zeros_like(done)


def finish_items_kernel(own, arrived, _, total):
    total[...] = own[...] + arrived[...]


def on_device(sizes, tiles, user_blocks, item_blocks, counts, user_factor, item_factor, week_factor):
    rows, groups = sizes
    chips = rows // 2
    tiles = tiles[0, 0]
    slots, weeks, height, width = tiles.shape
    rank = week_factor.shape[1]
    user_width = user_factor.shape[1]

    def limit(mebibytes):
        return pltpu.CompilerParams(vmem_limit_bytes=mebibytes << 20)

    product = pl.CostEstimate(
        flops=8 * slots * weeks * height * width * rank,
        bytes_accessed=4 * slots * weeks * height * width,
        transcendentals=0,
    )

    longer = pl.CostEstimate(
        flops=4 * product.flops, bytes_accessed=4 * product.bytes_accessed, transcendentals=0
    )

    def across_chips(value, step):
        return lax.ppermute(value, "users", [(i, i ^ (2 * step)) for i in range(rows)])

    def across_cores(value):
        return lax.ppermute(value, "users", [(i, i ^ 1) for i in range(rows)])

    def across_groups(value, step):
        return lax.ppermute(value, "items", [(i, i ^ step) for i in range(groups)])

    def array(*shape, dtype=F32):
        return jax.ShapeDtypeStruct(shape, dtype)

    sibling = across_cores(item_factor)
    asked = [item_blocks[0]] + [across_chips(item_blocks[0], step) for step in range(1, chips)]
    near = jnp.concatenate(asked, axis=0)
    far_users = across_groups(user_factor, groups // 2)
    *served, far_users = pl.pallas_call(
        functools.partial(serve_kernel, chips, width),
        out_shape=[array(rank, slots * width)] * (chips - 1) + [array(rank, user_width)],
        in_specs=[SMEM] + [VMEM] * 3,
        out_specs=[VMEM] * chips,
        compiler_params=limit(4),
        name="serve",
    )(near, item_factor, sibling, far_users)
    row_factors = {0: user_factor, groups // 2: far_users}
    step = groups // 4
    while step:
        row_factors |= {at ^ step: across_groups(v, step) for at, v in row_factors.items()}
        step //= 2
    messages = [across_chips(value, step + 1) for step, value in enumerate(served)]

    halves, spread = pl.pallas_call(
        prepare_kernel,
        out_shape=[
            array(slots, weeks, height, 2 * width, dtype=BF16),
            array(weeks, rank, height),
        ],
        in_specs=[SMEM, HBM, VMEM, ANY],
        out_specs=[VMEM] * 2,
        scratch_shapes=[
            pltpu.VMEM((slots, weeks, height, width), F32),
            pltpu.SemaphoreType.DMA((slots,)),
        ],
        compiler_params=limit(40),
        name="prepare",
    )(counts, tiles, week_factor, served[0])

    even, odd = pl.pallas_call(
        functools.partial(mode1_kernel, groups),
        out_shape=[array(groups // 2, rank, user_width)] * 2,
        in_specs=[SMEM] * 3 + [VMEM] * (3 + chips) + [ANY] * (groups - 1),
        out_specs=[VMEM] * 2,
        scratch_shapes=[pltpu.VMEM((groups * user_width // height, rank, height), F32)],
        compiler_params=limit(8),
        cost_estimate=product,
        name="mode1",
    )(
        counts,
        user_blocks[0],
        item_blocks[0],
        spread,
        halves,
        item_factor,
        sibling,
        *messages,
        *(row_factors[step] for step in range(1, groups)),
    )
    terms = pl.pallas_call(
        mode2_kernel,
        out_shape=array(rank, slots * width),
        in_specs=[SMEM] * 2 + [VMEM] * 2 + [ANY] + [VMEM] * groups,
        out_specs=VMEM,
        compiler_params=limit(8),
        cost_estimate=product,
        name="mode2",
    )(
        counts,
        user_blocks[0],
        spread,
        halves,
        even,
        *(row_factors[step] for step in range(groups)),
    )
    near_terms = [terms] + [across_chips(terms, step) for step in range(1, chips)]
    own, other = pl.pallas_call(
        collect_kernel,
        out_shape=[array(*item_factor.shape)] * 2,
        in_specs=[SMEM] + [VMEM] * chips,
        out_specs=[VMEM] * 2,
        compiler_params=limit(4),
        name="collect",
    )(near, *near_terms)
    kept, sent, step = even, odd, 1
    while step < groups // 2:
        arrived = across_groups(sent, step)
        kept, sent = kept[0::2] + arrived[0::2], kept[1::2] + arrived[1::2]
        step *= 2
    m_users, done = pl.pallas_call(
        finish_users_kernel,
        out_shape=[array(rank, user_width), array(8, 128)],
        in_specs=[VMEM] * 2,
        out_specs=[VMEM] * 2,
        compiler_params=limit(4),
        cost_estimate=longer,
        name="finish_users",
    )(kept[0], across_groups(sent[0], step))
    m_items = pl.pallas_call(
        finish_items_kernel,
        out_shape=array(*item_factor.shape),
        in_specs=[VMEM] * 2 + [ANY],
        out_specs=VMEM,
        compiler_params=limit(4),
        name="finish_items",
    )(own, across_cores(other), done)
    return m_users, m_items


def solution(mesh):
    rows, groups = mesh.shape["users"], mesh.shape["items"]
    assert rows > 1 and rows & (rows - 1) == 0 and groups > 1 and groups & (groups - 1) == 0
    return jax.shard_map(
        functools.partial(on_device, (rows, groups)),
        mesh=mesh,
        in_specs=(
            P("users", "items", None, None, None, None),
            P("users", "items", None),
            P("users", "items", None),
            P("users", "items"),
            P(None, ("users", "items")),
            P(None, ("items", "users")),
            P(),
        ),
        out_specs=(P(None, ("users", "items")), P(None, ("items", "users"))),
        check_vma=False,
    )
```

```python
import functools

import jax
import jax.numpy as jnp
from jax import lax
from jax.experimental import pallas as pl
from jax.experimental.pallas import tpu as pltpu
from jax.sharding import PartitionSpec as P

F32 = jnp.float32
BF16 = jnp.bfloat16
ANY = pl.BlockSpec(memory_space=pl.ANY)
HBM = pl.BlockSpec(memory_space=pltpu.HBM)
SMEM = pl.BlockSpec(memory_space=pltpu.SMEM)
VMEM = pl.BlockSpec(memory_space=pltpu.VMEM)


def columns(block, width):
    return pl.ds(pl.multiple_of(block * width, width), width)


def split(value):
    high = value.astype(BF16)
    return high, (value - high.astype(F32)).astype(BF16)


def hold_kernel(item_factor, week_factor, items, spread, doubled):
    items[...] = item_factor[...]
    doubled[...] = jnp.concatenate([week_factor[...]] * 2, axis=1)
    weeks_t = week_factor[...].T
    for week in range(spread.shape[0]):
        spread[week] = jnp.broadcast_to(weeks_t[:, week : week + 1], spread.shape[1:])


def prepare_kernel(count_ref, tiles, _, halves, held, sems):
    slots, weeks, height, width = tiles.shape
    count = count_ref[0, 0]

    def fetch(slot):
        return pltpu.make_async_copy(tiles.at[slot], held.at[slot], sems.at[slot])

    for slot in range(slots):

        @pl.when(slot < count)
        def _():
            fetch(slot).start()

    def work(slot, carry):
        fetch(slot).wait()

        def one(week, inner):
            high, low = split(held[slot, week])
            halves[slot, week, :, :width] = high
            halves[slot, week, :, width:] = low
            return inner

        return lax.fori_loop(0, weeks, one, carry, unroll=8)

    lax.fori_loop(0, count, work, 0)


def serve_kernel(chips, width, requests, own, sibling, users, *refs):
    *messages, users_out = refs
    users_out[...] = users[...]
    me = lax.axis_index("users")
    per_device = own.shape[1] // width
    for step in range(1, chips):
        for slot in range(requests.shape[1]):
            index = requests[step, slot]
            device = index // per_device
            place = columns(index % per_device, width)
            for owner, source in ((me, own), (me ^ 1, sibling)):

                @pl.when(device == owner)
                def _():
                    messages[step - 1][:, slot * width : (slot + 1) * width] = source[:, place]


def user_term(doubled, items, tile, together=4):
    weeks, height, width = tile.shape
    rank = items.shape[0]
    high, low = split(items)
    both = jnp.concatenate([high.astype(F32), low.astype(F32)], axis=0).T.astype(BF16)
    both = jnp.concatenate([both, both], axis=0)
    total = jnp.zeros((height, 2 * rank), F32)
    for week in range(0, weeks, together):
        rows = tile[week : week + together].reshape(together * height, width)
        sums = jnp.dot(rows, both, preferred_element_type=F32)
        for part in range(together):
            total += sums[part * height : (part + 1) * height] * doubled[week + part, :][None]
    total = total.T
    return total[:rank] + total[rank:]


def item_term(spread, users, tile):
    weeks, height, width = tile.shape
    width //= 2
    rank = users.shape[0]
    total = jnp.zeros((2 * rank, 2 * width), F32)
    for week in range(0, weeks, 2):
        left = [
            jnp.concatenate(split(spread[part] * users), axis=0) for part in (week, week + 1)
        ]
        total += jnp.dot(
            jnp.concatenate(left, axis=1),
            jnp.concatenate([tile[week], tile[week + 1]], axis=0),
            preferred_element_type=F32,
        )
    half = total[:rank] + total[rank:]
    return half[:, :width] + half[:, width:]


def mode1_kernel(groups, count_ref, users_ref, items_ref, doubled, tiles, own, sibling, *refs):
    messages, (even, odd, sums) = refs[: -2 - groups], refs[-3:]
    height, width = tiles.shape[2], tiles.shape[3] // 2
    me = lax.axis_index("users")
    column = lax.axis_index("items")
    per_device = own.shape[1] // width
    kept = even.shape[2] // height
    sums[...] = jnp.zeros_like(sums)

    def work(slot, carry):
        index = items_ref[0, slot]
        device = index // per_device
        place = columns(index % per_device, width)
        items = jnp.where(device == me, own[:, place], sibling[:, place])
        source = (device // 2) ^ (me // 2)
        here = columns(slot, width)
        for step, message in enumerate(messages):
            items = jnp.where(source == step + 1, message[:, here], items)
        sums[users_ref[0, slot]] += user_term(doubled, items, tiles.at[slot])
        return carry

    lax.fori_loop(0, count_ref[0, 0], work, 0)
    for step in range(groups):
        first = (column ^ step) * kept
        for block in range(kept):
            target = (even, odd)[step % 2]
            target[step // 2, :, block * height : (block + 1) * height] = sums[first + block]


def mode2_kernel(count_ref, users_ref, spread, tiles, _, *refs):
    *factors, terms = refs
    height, width = tiles.shape[2], tiles.shape[3] // 2
    column = lax.axis_index("items")
    kept = factors[0].shape[1] // height
    terms[...] = jnp.zeros_like(terms)

    def work(slot, carry):
        block = users_ref[0, slot]
        source = (block // kept) ^ column
        place = columns(block % kept, height)
        users = factors[0][:, place]
        for step in range(1, len(factors)):
            users = jnp.where(source == step, factors[step][:, place], users)
        terms[:, columns(slot, width)] = item_term(spread, users, tiles.at[slot])
        return carry

    lax.fori_loop(0, count_ref[0, 0], work, 0)


def collect_kernel(ids, *refs):
    *terms, own, other = refs
    slots = ids.shape[1]
    width = terms[0].shape[1] // slots
    per_device = own.shape[1] // width
    me = lax.axis_index("users")
    own[...] = jnp.zeros_like(own)
    other[...] = jnp.zeros_like(other)
    for step, term in enumerate(terms):
        for slot in range(slots):
            index = ids[step, slot]
            device = index // per_device
            place = columns(index % per_device, width)
            for owner, target in ((me, own), (me ^ 1, other)):

                @pl.when(device == owner)
                def _():
                    target[:, place] += term[:, slot * width : (slot + 1) * width]


def finish_users_kernel(kept, arrived, total, done):
    total[...] = kept[...] + arrived[...]
    done[...] = jnp.zeros_like(done)


def finish_items_kernel(own, arrived, _, total):
    total[...] = own[...] + arrived[...]


def on_device(sizes, tiles, user_blocks, item_blocks, counts, user_factor, item_factor, week_factor):
    rows, groups = sizes
    chips = rows // 2
    tiles = tiles[0, 0]
    slots, weeks, height, width = tiles.shape
    rank = week_factor.shape[1]
    user_width = user_factor.shape[1]

    def limit(mebibytes):
        return pltpu.CompilerParams(vmem_limit_bytes=mebibytes << 20)

    product = pl.CostEstimate(
        flops=8 * slots * weeks * height * width * rank,
        bytes_accessed=4 * slots * weeks * height * width,
        transcendentals=0,
    )

    longer = pl.CostEstimate(
        flops=4 * product.flops, bytes_accessed=4 * product.bytes_accessed, transcendentals=0
    )

    def across_chips(value, step):
        return lax.ppermute(value, "users", [(i, i ^ (2 * step)) for i in range(rows)])

    def across_cores(value):
        return lax.ppermute(value, "users", [(i, i ^ 1) for i in range(rows)])

    def across_groups(value, step):
        return lax.ppermute(value, "items", [(i, i ^ step) for i in range(groups)])

    def array(*shape, dtype=F32):
        return jax.ShapeDtypeStruct(shape, dtype)

    sibling = across_cores(item_factor)
    asked = [item_blocks[0]] + [across_chips(item_blocks[0], step) for step in range(1, chips)]
    near = jnp.concatenate(asked, axis=0)
    far_users = across_groups(user_factor, groups // 2)
    here, spread, doubled = pl.pallas_call(
        hold_kernel,
        out_shape=[
            array(*item_factor.shape),
            array(weeks, rank, height),
            array(weeks, 2 * rank),
        ],
        in_specs=[VMEM] * 2,
        out_specs=[VMEM] * 3,
        compiler_params=limit(4),
        name="hold",
    )(item_factor, week_factor)

    *served, far_users = pl.pallas_call(
        functools.partial(serve_kernel, chips, width),
        out_shape=[array(rank, slots * width)] * (chips - 1) + [array(rank, user_width)],
        in_specs=[SMEM] + [VMEM] * 3,
        out_specs=[VMEM] * chips,
        compiler_params=limit(4),
        name="serve",
    )(near, here, sibling, far_users)
    row_factors = {0: user_factor, groups // 2: far_users}
    step = groups // 4
    while step:
        row_factors |= {at ^ step: across_groups(v, step) for at, v in row_factors.items()}
        step //= 2
    messages = [across_chips(value, step + 1) for step, value in enumerate(served)]

    halves = pl.pallas_call(
        prepare_kernel,
        out_shape=array(slots, weeks, height, 2 * width, dtype=BF16),
        in_specs=[SMEM, HBM, ANY],
        out_specs=VMEM,
        scratch_shapes=[
            pltpu.VMEM((slots, weeks, height, width), F32),
            pltpu.SemaphoreType.DMA((slots,)),
        ],
        compiler_params=limit(40),
        name="prepare",
    )(counts, tiles, served[0])

    even, odd = pl.pallas_call(
        functools.partial(mode1_kernel, groups),
        out_shape=[array(groups // 2, rank, user_width)] * 2,
        in_specs=[SMEM] * 3 + [VMEM] * (3 + chips) + [ANY] * (groups - 1),
        out_specs=[VMEM] * 2,
        scratch_shapes=[pltpu.VMEM((groups * user_width // height, rank, height), F32)],
        compiler_params=limit(8),
        cost_estimate=product,
        name="mode1",
    )(
        counts,
        user_blocks[0],
        item_blocks[0],
        doubled,
        halves,
        here,
        sibling,
        *messages,
        *(row_factors[step] for step in range(1, groups)),
    )
    terms = pl.pallas_call(
        mode2_kernel,
        out_shape=array(rank, slots * width),
        in_specs=[SMEM] * 2 + [VMEM] * 2 + [ANY] + [VMEM] * groups,
        out_specs=VMEM,
        compiler_params=limit(8),
        cost_estimate=product,
        name="mode2",
    )(
        counts,
        user_blocks[0],
        spread,
        halves,
        even,
        *(row_factors[step] for step in range(groups)),
    )
    near_terms = [terms] + [across_chips(terms, step) for step in range(1, chips)]
    own, other = pl.pallas_call(
        collect_kernel,
        out_shape=[array(*item_factor.shape)] * 2,
        in_specs=[SMEM] + [VMEM] * chips,
        out_specs=[VMEM] * 2,
        compiler_params=limit(4),
        name="collect",
    )(near, *near_terms)
    kept, sent, step = even, odd, 1
    while step < groups // 2:
        arrived = across_groups(sent, step)
        kept, sent = kept[0::2] + arrived[0::2], kept[1::2] + arrived[1::2]
        step *= 2
    m_users, done = pl.pallas_call(
        finish_users_kernel,
        out_shape=[array(rank, user_width), array(8, 128)],
        in_specs=[VMEM] * 2,
        out_specs=[VMEM] * 2,
        compiler_params=limit(4),
        cost_estimate=longer,
        name="finish_users",
    )(kept[0], across_groups(sent[0], step))
    m_items = pl.pallas_call(
        finish_items_kernel,
        out_shape=array(*item_factor.shape),
        in_specs=[VMEM] * 2 + [ANY],
        out_specs=VMEM,
        compiler_params=limit(4),
        name="finish_items",
    )(own, across_cores(other), done)
    return m_users, m_items


def solution(mesh):
    rows, groups = mesh.shape["users"], mesh.shape["items"]
    assert rows > 1 and rows & (rows - 1) == 0 and groups > 1 and groups & (groups - 1) == 0
    return jax.shard_map(
        functools.partial(on_device, (rows, groups)),
        mesh=mesh,
        in_specs=(
            P("users", "items", None, None, None, None),
            P("users", "items", None),
            P("users", "items", None),
            P("users", "items"),
            P(None, ("users", "items")),
            P(None, ("items", "users")),
            P(),
        ),
        out_specs=(P(None, ("users", "items")), P(None, ("items", "users"))),
        check_vma=False,
    )
```

```python
import functools

import jax
import jax.numpy as jnp
from jax import lax
from jax.experimental import pallas as pl
from jax.experimental.pallas import tpu as pltpu
from jax.sharding import PartitionSpec as P

F32 = jnp.float32
BF16 = jnp.bfloat16
ANY = pl.BlockSpec(memory_space=pl.ANY)
HBM = pl.BlockSpec(memory_space=pltpu.HBM)
SMEM = pl.BlockSpec(memory_space=pltpu.SMEM)
VMEM = pl.BlockSpec(memory_space=pltpu.VMEM)


def columns(block, width):
    return pl.ds(pl.multiple_of(block * width, width), width)


def split(value):
    high = value.astype(BF16)
    return high, (value - high.astype(F32)).astype(BF16)


def hold_kernel(item_factor, week_factor, items, spread):
    items[...] = item_factor[...]
    weeks_t = week_factor[...].T
    for week in range(spread.shape[0]):
        spread[week] = jnp.broadcast_to(weeks_t[:, week : week + 1], spread.shape[1:])


def prepare_kernel(ids, tiles, _, halves, held, sems):
    slots, weeks, height, width = tiles.shape
    count = ids[ids.shape[0] - 1, 0]

    def fetch(slot):
        return pltpu.make_async_copy(tiles.at[slot], held.at[slot], sems.at[slot])

    for slot in range(slots):

        @pl.when(slot < count)
        def _():
            fetch(slot).start()

    def work(slot, carry):
        fetch(slot).wait()

        def one(week, inner):
            high, low = split(held[slot, week])
            halves[slot, week, :, :width] = high
            halves[slot, week, :, width:] = low
            return inner

        return lax.fori_loop(0, weeks, one, carry, unroll=8)

    lax.fori_loop(0, count, work, 0)


def serve_kernel(chips, width, ids, own, sibling, users, *refs):
    *messages, users_out = refs
    users_out[...] = users[...]
    me = lax.axis_index("users")
    per_device = own.shape[1] // width
    for step in range(1, chips):
        for slot in range(ids.shape[1]):
            index = ids[step, slot]
            device = index // per_device
            place = columns(index % per_device, width)
            for owner, source in ((me, own), (me ^ 1, sibling)):

                @pl.when(device == owner)
                def _():
                    messages[step - 1][:, slot * width : (slot + 1) * width] = source[:, place]


def user_term(spread, items, tile, together=8):
    weeks, height, width = tile.shape
    rank = items.shape[0]
    both = jnp.concatenate(split(items), axis=0)
    both = jnp.concatenate([both, both], axis=1)
    total = jnp.zeros((rank, height), F32)
    for week in range(0, weeks, together):
        rows = tile[week : week + together].reshape(together * height, width)
        sums = lax.dot_general(both, rows, (((1,), (1,)), ((), ())), preferred_element_type=F32)
        for part in range(together):
            here = sums[:, part * height : (part + 1) * height]
            total += (here[:rank] + here[rank:]) * spread[week + part]
    return total


def item_term(spread, users, tile):
    weeks, height, width = tile.shape
    width //= 2
    rank = users.shape[0]
    total = jnp.zeros((2 * rank, 2 * width), F32)
    for week in range(0, weeks, 2):
        left = [
            jnp.concatenate(split(spread[part] * users), axis=0) for part in (week, week + 1)
        ]
        total += jnp.dot(
            jnp.concatenate(left, axis=1),
            jnp.concatenate([tile[week], tile[week + 1]], axis=0),
            preferred_element_type=F32,
        )
    half = total[:rank] + total[rank:]
    return half[:, :width] + half[:, width:]


def mode1_kernel(groups, ids, spread, tiles, own, sibling, *refs):
    messages, (even, odd, sums) = refs[: -2 - groups], refs[-3:]
    height, width = tiles.shape[2], tiles.shape[3] // 2
    me = lax.axis_index("users")
    column = lax.axis_index("items")
    per_device = own.shape[1] // width
    kept = even.shape[2] // height
    sums[...] = jnp.zeros_like(sums)

    def work(slot, carry):
        index = ids[0, slot]
        device = index // per_device
        place = columns(index % per_device, width)
        items = jnp.where(device == me, own[:, place], sibling[:, place])
        source = (device // 2) ^ (me // 2)
        here = columns(slot, width)
        for step, message in enumerate(messages):
            items = jnp.where(source == step + 1, message[:, here], items)
        sums[ids[ids.shape[0] - 2, slot]] += user_term(spread, items, tiles.at[slot])
        return carry

    lax.fori_loop(0, ids[ids.shape[0] - 1, 0], work, 0)
    for step in range(groups):
        first = (column ^ step) * kept
        for block in range(kept):
            target = (even, odd)[step % 2]
            target[step // 2, :, block * height : (block + 1) * height] = sums[first + block]


def mode2_kernel(ids, spread, tiles, _, *refs):
    *factors, terms = refs
    height, width = tiles.shape[2], tiles.shape[3] // 2
    column = lax.axis_index("items")
    kept = factors[0].shape[1] // height
    terms[...] = jnp.zeros_like(terms)

    def work(slot, carry):
        block = ids[ids.shape[0] - 2, slot]
        source = (block // kept) ^ column
        place = columns(block % kept, height)
        users = factors[0][:, place]
        for step in range(1, len(factors)):
            users = jnp.where(source == step, factors[step][:, place], users)
        terms[:, columns(slot, width)] = item_term(spread, users, tiles.at[slot])
        return carry

    lax.fori_loop(0, ids[ids.shape[0] - 1, 0], work, 0)


def collect_kernel(ids, *refs):
    *terms, own, other = refs
    slots = ids.shape[1]
    width = terms[0].shape[1] // slots
    per_device = own.shape[1] // width
    me = lax.axis_index("users")
    own[...] = jnp.zeros_like(own)
    other[...] = jnp.zeros_like(other)
    for step, term in enumerate(terms):
        for slot in range(slots):
            index = ids[step, slot]
            device = index // per_device
            place = columns(index % per_device, width)
            for owner, target in ((me, own), (me ^ 1, other)):

                @pl.when(device == owner)
                def _():
                    target[:, place] += term[:, slot * width : (slot + 1) * width]


def finish_users_kernel(kept, arrived, total, done):
    total[...] = kept[...] + arrived[...]
    done[...] = jnp.zeros_like(done)


def finish_items_kernel(own, arrived, _, total):
    total[...] = own[...] + arrived[...]


def on_device(sizes, tiles, user_blocks, item_blocks, counts, user_factor, item_factor, week_factor):
    rows, groups = sizes
    chips = rows // 2
    tiles = tiles[0, 0]
    slots, weeks, height, width = tiles.shape
    rank = week_factor.shape[1]
    user_width = user_factor.shape[1]

    def limit(mebibytes):
        return pltpu.CompilerParams(vmem_limit_bytes=mebibytes << 20)

    product = pl.CostEstimate(
        flops=8 * slots * weeks * height * width * rank,
        bytes_accessed=4 * slots * weeks * height * width,
        transcendentals=0,
    )

    longer = pl.CostEstimate(
        flops=4 * product.flops, bytes_accessed=4 * product.bytes_accessed, transcendentals=0
    )

    def across_chips(value, step):
        return lax.ppermute(value, "users", [(i, i ^ (2 * step)) for i in range(rows)])

    def across_cores(value):
        return lax.ppermute(value, "users", [(i, i ^ 1) for i in range(rows)])

    def across_groups(value, step):
        return lax.ppermute(value, "items", [(i, i ^ step) for i in range(groups)])

    def array(*shape, dtype=F32):
        return jax.ShapeDtypeStruct(shape, dtype)

    sibling = across_cores(item_factor)
    asked = [item_blocks[0]] + [across_chips(item_blocks[0], step) for step in range(1, chips)]
    counted = jnp.pad(counts, ((0, 0), (0, slots - 1)))
    ids = jnp.concatenate([*asked, user_blocks[0], counted], axis=0)
    far_users = across_groups(user_factor, groups // 2)
    here, spread = pl.pallas_call(
        hold_kernel,
        out_shape=[
            array(*item_factor.shape),
            array(weeks, rank, height),
        ],
        in_specs=[VMEM] * 2,
        out_specs=[VMEM] * 2,
        compiler_params=limit(4),
        name="hold",
    )(item_factor, week_factor)

    *served, far_users = pl.pallas_call(
        functools.partial(serve_kernel, chips, width),
        out_shape=[array(rank, slots * width)] * (chips - 1) + [array(rank, user_width)],
        in_specs=[SMEM] + [VMEM] * 3,
        out_specs=[VMEM] * chips,
        compiler_params=limit(4),
        name="serve",
    )(ids, here, sibling, far_users)
    row_factors = {0: user_factor, groups // 2: far_users}
    step = groups // 4
    while step:
        row_factors |= {at ^ step: across_groups(v, step) for at, v in row_factors.items()}
        step //= 2
    messages = [across_chips(value, step + 1) for step, value in enumerate(served)]

    halves = pl.pallas_call(
        prepare_kernel,
        out_shape=array(slots, weeks, height, 2 * width, dtype=BF16),
        in_specs=[SMEM, HBM, ANY],
        out_specs=VMEM,
        scratch_shapes=[
            pltpu.VMEM((slots, weeks, height, width), F32),
            pltpu.SemaphoreType.DMA((slots,)),
        ],
        compiler_params=limit(40),
        name="prepare",
    )(ids, tiles, served[0])

    even, odd = pl.pallas_call(
        functools.partial(mode1_kernel, groups),
        out_shape=[array(groups // 2, rank, user_width)] * 2,
        in_specs=[SMEM] + [VMEM] * (3 + chips) + [ANY] * (groups - 1),
        out_specs=[VMEM] * 2,
        scratch_shapes=[pltpu.VMEM((groups * user_width // height, rank, height), F32)],
        compiler_params=limit(8),
        cost_estimate=product,
        name="mode1",
    )(
        ids,
        spread,
        halves,
        here,
        sibling,
        *messages,
        *(row_factors[step] for step in range(1, groups)),
    )
    terms = pl.pallas_call(
        mode2_kernel,
        out_shape=array(rank, slots * width),
        in_specs=[SMEM] + [VMEM] * 2 + [ANY] + [VMEM] * groups,
        out_specs=VMEM,
        compiler_params=limit(8),
        cost_estimate=product,
        name="mode2",
    )(
        ids,
        spread,
        halves,
        even,
        *(row_factors[step] for step in range(groups)),
    )
    near_terms = [terms] + [across_chips(terms, step) for step in range(1, chips)]
    own, other = pl.pallas_call(
        collect_kernel,
        out_shape=[array(*item_factor.shape)] * 2,
        in_specs=[SMEM] + [VMEM] * chips,
        out_specs=[VMEM] * 2,
        compiler_params=limit(4),
        name="collect",
    )(ids, *near_terms)
    kept, sent, step = even, odd, 1
    while step < groups // 2:
        arrived = across_groups(sent, step)
        kept, sent = kept[0::2] + arrived[0::2], kept[1::2] + arrived[1::2]
        step *= 2
    m_users, done = pl.pallas_call(
        finish_users_kernel,
        out_shape=[array(rank, user_width), array(8, 128)],
        in_specs=[VMEM] * 2,
        out_specs=[VMEM] * 2,
        compiler_params=limit(4),
        cost_estimate=longer,
        name="finish_users",
    )(kept[0], across_groups(sent[0], step))
    m_items = pl.pallas_call(
        finish_items_kernel,
        out_shape=array(*item_factor.shape),
        in_specs=[VMEM] * 2 + [ANY],
        out_specs=VMEM,
        compiler_params=limit(4),
        name="finish_items",
    )(own, across_cores(other), done)
    return m_users, m_items


def solution(mesh):
    rows, groups = mesh.shape["users"], mesh.shape["items"]
    assert rows > 1 and rows & (rows - 1) == 0 and groups > 1 and groups & (groups - 1) == 0
    return jax.shard_map(
        functools.partial(on_device, (rows, groups)),
        mesh=mesh,
        in_specs=(
            P("users", "items", None, None, None, None),
            P("users", "items", None),
            P("users", "items", None),
            P("users", "items"),
            P(None, ("users", "items")),
            P(None, ("items", "users")),
            P(),
        ),
        out_specs=(P(None, ("users", "items")), P(None, ("items", "users"))),
        check_vma=False,
    )
```

```python
import functools

import jax
import jax.numpy as jnp
from jax import lax
from jax.experimental import pallas as pl
from jax.experimental.pallas import tpu as pltpu
from jax.sharding import PartitionSpec as P

F32 = jnp.float32
BF16 = jnp.bfloat16
ANY = pl.BlockSpec(memory_space=pl.ANY)
HBM = pl.BlockSpec(memory_space=pltpu.HBM)
SMEM = pl.BlockSpec(memory_space=pltpu.SMEM)
VMEM = pl.BlockSpec(memory_space=pltpu.VMEM)


def columns(block, width):
    return pl.ds(pl.multiple_of(block * width, width), width)


def split(value):
    high = value.astype(BF16)
    return high, (value - high.astype(F32)).astype(BF16)


def hold_kernel(done):
    done[...] = jnp.zeros_like(done)


def prepare_kernel(count_ref, tiles, week_factor, users, _, halves, spread, users_out):
    weeks, width = tiles.shape[1], tiles.shape[3]
    users_out[...] = users[...]
    weeks_t = week_factor[...].T
    for week in range(weeks):
        spread[week] = jnp.broadcast_to(weeks_t[:, week : week + 1], spread.shape[1:])

    def work(slot, carry):
        def one(week, inner):
            high, low = split(tiles[slot, week])
            halves[slot, week, :, :width] = high
            halves[slot, week, :, width:] = low
            return inner

        return lax.fori_loop(0, weeks, one, carry, unroll=8)

    lax.fori_loop(0, count_ref[0, 0], work, 0)


def serve_kernel(chips, width, requests, own, sibling, _, *messages):
    me = lax.axis_index("users")
    per_device = own.shape[1] // width
    for step in range(1, chips):
        for slot in range(requests.shape[1]):
            index = requests[step, slot]
            device = index // per_device
            place = columns(index % per_device, width)
            for owner, source in ((me, own), (me ^ 1, sibling)):

                @pl.when(device == owner)
                def _():
                    messages[step - 1][:, slot * width : (slot + 1) * width] = source[:, place]


def user_term(spread, items, tile, together=8):
    weeks, height, width = tile.shape
    rank = items.shape[0]
    both = jnp.concatenate(split(items), axis=0)
    both = jnp.concatenate([both, both], axis=1)
    total = jnp.zeros((rank, height), F32)
    for week in range(0, weeks, together):
        rows = tile[week : week + together].reshape(together * height, width)
        sums = lax.dot_general(both, rows, (((1,), (1,)), ((), ())), preferred_element_type=F32)
        for part in range(together):
            here = sums[:, part * height : (part + 1) * height]
            total += (here[:rank] + here[rank:]) * spread[week + part]
    return total


def item_term(spread, users, tile):
    weeks, height, width = tile.shape
    width //= 2
    rank = users.shape[0]
    total = jnp.zeros((2 * rank, 2 * width), F32)
    for week in range(0, weeks, 2):
        left = [
            jnp.concatenate(split(spread[part] * users), axis=0) for part in (week, week + 1)
        ]
        total += jnp.dot(
            jnp.concatenate(left, axis=1),
            jnp.concatenate([tile[week], tile[week + 1]], axis=0),
            preferred_element_type=F32,
        )
    half = total[:rank] + total[rank:]
    return half[:, :width] + half[:, width:]


def mode1_kernel(groups, count_ref, users_ref, items_ref, spread, tiles, own, sibling, *refs):
    messages, (even, odd, sums) = refs[: -2 - groups], refs[-3:]
    height, width = tiles.shape[2], tiles.shape[3] // 2
    me = lax.axis_index("users")
    column = lax.axis_index("items")
    per_device = own.shape[1] // width
    kept = even.shape[2] // height
    sums[...] = jnp.zeros_like(sums)

    def work(slot, carry):
        index = items_ref[0, slot]
        device = index // per_device
        place = columns(index % per_device, width)
        items = jnp.where(device == me, own[:, place], sibling[:, place])
        source = (device // 2) ^ (me // 2)
        here = columns(slot, width)
        for step, message in enumerate(messages):
            items = jnp.where(source == step + 1, message[:, here], items)
        sums[users_ref[0, slot]] += user_term(spread, items, tiles.at[slot])
        return carry

    lax.fori_loop(0, count_ref[0, 0], work, 0)
    for step in range(groups):
        first = (column ^ step) * kept
        for block in range(kept):
            target = (even, odd)[step % 2]
            target[step // 2, :, block * height : (block + 1) * height] = sums[first + block]


def mode2_kernel(count_ref, users_ref, spread, tiles, _, *refs):
    *factors, terms = refs
    height, width = tiles.shape[2], tiles.shape[3] // 2
    column = lax.axis_index("items")
    kept = factors[0].shape[1] // height
    terms[...] = jnp.zeros_like(terms)

    def work(slot, carry):
        block = users_ref[0, slot]
        source = (block // kept) ^ column
        place = columns(block % kept, height)
        users = factors[0][:, place]
        for step in range(1, len(factors)):
            users = jnp.where(source == step, factors[step][:, place], users)
        terms[:, columns(slot, width)] = item_term(spread, users, tiles.at[slot])
        return carry

    lax.fori_loop(0, count_ref[0, 0], work, 0)


def collect_kernel(ids, *refs):
    *terms, own, other = refs
    slots = ids.shape[1]
    width = terms[0].shape[1] // slots
    per_device = own.shape[1] // width
    me = lax.axis_index("users")
    own[...] = jnp.zeros_like(own)
    other[...] = jnp.zeros_like(other)
    for step, term in enumerate(terms):
        for slot in range(slots):
            index = ids[step, slot]
            device = index // per_device
            place = columns(index % per_device, width)
            for owner, target in ((me, own), (me ^ 1, other)):

                @pl.when(device == owner)
                def _():
                    target[:, place] += term[:, slot * width : (slot + 1) * width]


def finish_users_kernel(kept, arrived, total, done):
    total[...] = kept[...] + arrived[...]
    done[...] = jnp.zeros_like(done)


def finish_items_kernel(own, arrived, _, total):
    total[...] = own[...] + arrived[...]


def on_device(sizes, tiles, user_blocks, item_blocks, counts, user_factor, item_factor, week_factor):
    rows, groups = sizes
    chips = rows // 2
    tiles = tiles[0, 0]
    slots, weeks, height, width = tiles.shape
    rank = week_factor.shape[1]
    user_width = user_factor.shape[1]

    def limit(mebibytes):
        return pltpu.CompilerParams(vmem_limit_bytes=mebibytes << 20)

    def cost(times):
        return pl.CostEstimate(
            flops=int(times * 8 * slots * weeks * height * width * rank),
            bytes_accessed=int(times * 4 * slots * weeks * height * width),
            transcendentals=0,
        )

    def across_chips(value, step):
        return lax.ppermute(value, "users", [(i, i ^ (2 * step)) for i in range(rows)])

    def across_cores(value):
        return lax.ppermute(value, "users", [(i, i ^ 1) for i in range(rows)])

    def across_groups(value, step):
        return lax.ppermute(value, "items", [(i, i ^ step) for i in range(groups)])

    def array(*shape, dtype=F32):
        return jax.ShapeDtypeStruct(shape, dtype)

    sibling = across_cores(item_factor)
    asked = [item_blocks[0]] + [across_chips(item_blocks[0], step) for step in range(1, chips)]
    near = jnp.concatenate(asked, axis=0)
    far_users = across_groups(user_factor, groups // 2)
    held = pl.pallas_call(
        hold_kernel,
        out_shape=array(8, 128),
        out_specs=VMEM,
        compiler_params=limit(4),
        cost_estimate=cost(4),
        name="hold",
    )()

    served = pl.pallas_call(
        functools.partial(serve_kernel, chips, width),
        out_shape=[array(rank, slots * width)] * (chips - 1),
        in_specs=[SMEM] + [VMEM] * 2 + [ANY],
        out_specs=[VMEM] * (chips - 1),
        compiler_params=limit(4),
        cost_estimate=cost(1),
        name="serve",
    )(near, item_factor, sibling, held)
    messages = [across_chips(value, step + 1) for step, value in enumerate(served)]

    halves, spread, far_users = pl.pallas_call(
        prepare_kernel,
        out_shape=[
            array(slots, weeks, height, 2 * width, dtype=BF16),
            array(weeks, rank, height),
            array(rank, user_width),
        ],
        in_specs=[SMEM] + [VMEM] * 3 + [ANY],
        out_specs=[VMEM] * 3,
        compiler_params=limit(24),
        name="prepare",
    )(counts, tiles, week_factor, far_users, served[0])
    row_factors = {0: user_factor, groups // 2: far_users}
    step = groups // 4
    while step:
        row_factors |= {at ^ step: across_groups(v, step) for at, v in row_factors.items()}
        step //= 2

    even, odd = pl.pallas_call(
        functools.partial(mode1_kernel, groups),
        out_shape=[array(groups // 2, rank, user_width)] * 2,
        in_specs=[SMEM] * 3 + [VMEM] * (3 + chips) + [ANY] * (groups - 1),
        out_specs=[VMEM] * 2,
        scratch_shapes=[pltpu.VMEM((groups * user_width // height, rank, height), F32)],
        compiler_params=limit(8),
        cost_estimate=cost(1),
        name="mode1",
    )(
        counts,
        user_blocks[0],
        item_blocks[0],
        spread,
        halves,
        item_factor,
        sibling,
        *messages,
        *(row_factors[step] for step in range(1, groups)),
    )
    terms = pl.pallas_call(
        mode2_kernel,
        out_shape=array(rank, slots * width),
        in_specs=[SMEM] * 2 + [VMEM] * 2 + [ANY] + [VMEM] * groups,
        out_specs=VMEM,
        compiler_params=limit(8),
        cost_estimate=cost(1),
        name="mode2",
    )(
        counts,
        user_blocks[0],
        spread,
        halves,
        even,
        *(row_factors[step] for step in range(groups)),
    )
    near_terms = [terms] + [across_chips(terms, step) for step in range(1, chips)]
    own, other = pl.pallas_call(
        collect_kernel,
        out_shape=[array(*item_factor.shape)] * 2,
        in_specs=[SMEM] + [VMEM] * chips,
        out_specs=[VMEM] * 2,
        compiler_params=limit(4),
        name="collect",
    )(near, *near_terms)
    kept, sent, step = even, odd, 1
    while step < groups // 2:
        arrived = across_groups(sent, step)
        kept, sent = kept[0::2] + arrived[0::2], kept[1::2] + arrived[1::2]
        step *= 2
    m_users, done = pl.pallas_call(
        finish_users_kernel,
        out_shape=[array(rank, user_width), array(8, 128)],
        in_specs=[VMEM] * 2,
        out_specs=[VMEM] * 2,
        compiler_params=limit(4),
        cost_estimate=cost(4),
        name="finish_users",
    )(kept[0], across_groups(sent[0], step))
    m_items = pl.pallas_call(
        finish_items_kernel,
        out_shape=array(*item_factor.shape),
        in_specs=[VMEM] * 2 + [ANY],
        out_specs=VMEM,
        compiler_params=limit(4),
        name="finish_items",
    )(own, across_cores(other), done)
    return m_users, m_items


def solution(mesh):
    rows, groups = mesh.shape["users"], mesh.shape["items"]
    assert rows > 1 and rows & (rows - 1) == 0 and groups > 1 and groups & (groups - 1) == 0
    return jax.shard_map(
        functools.partial(on_device, (rows, groups)),
        mesh=mesh,
        in_specs=(
            P("users", "items", None, None, None, None),
            P("users", "items", None),
            P("users", "items", None),
            P("users", "items"),
            P(None, ("users", "items")),
            P(None, ("items", "users")),
            P(),
        ),
        out_specs=(P(None, ("users", "items")), P(None, ("items", "users"))),
        check_vma=False,
    )
```

```python
import functools

import jax
import jax.numpy as jnp
from jax import lax
from jax.experimental import pallas as pl
from jax.experimental.pallas import tpu as pltpu
from jax.sharding import PartitionSpec as P

F32 = jnp.float32
BF16 = jnp.bfloat16
ANY = pl.BlockSpec(memory_space=pl.ANY)
HBM = pl.BlockSpec(memory_space=pltpu.HBM)
SMEM = pl.BlockSpec(memory_space=pltpu.SMEM)
VMEM = pl.BlockSpec(memory_space=pltpu.VMEM)


def columns(block, width):
    return pl.ds(pl.multiple_of(block * width, width), width)


def split(value):
    high = value.astype(BF16)
    return high, (value - high.astype(F32)).astype(BF16)


def hold_kernel(done):
    done[...] = jnp.zeros_like(done)


def prepare_kernel(count_ref, tiles, week_factor, users, _, halves, spread, users_out):
    weeks, width = tiles.shape[1], tiles.shape[3]
    users_out[...] = users[...]
    weeks_t = week_factor[...].T
    for week in range(weeks):
        spread[week] = jnp.broadcast_to(weeks_t[:, week : week + 1], spread.shape[1:])

    def work(slot, carry):
        def one(week, inner):
            high, low = split(tiles[slot, week])
            halves[slot, week, :, :width] = high
            halves[slot, week, :, width:] = low
            return inner

        return lax.fori_loop(0, weeks, one, carry, unroll=8)

    lax.fori_loop(0, count_ref[0, 0], work, 0)


def serve_kernel(chips, width, requests, own, sibling, _, *messages):
    me = lax.axis_index("users")
    per_device = own.shape[1] // width
    for step in range(1, chips):
        for slot in range(requests.shape[1]):
            index = requests[step, slot]
            device = index // per_device
            place = columns(index % per_device, width)
            for owner, source in ((me, own), (me ^ 1, sibling)):

                @pl.when(device == owner)
                def _():
                    messages[step - 1][:, slot * width : (slot + 1) * width] = source[:, place]


def user_term(spread, items, tile, together=8):
    weeks, height, width = tile.shape
    rank = items.shape[0]
    both = jnp.concatenate(split(items), axis=0)
    both = jnp.concatenate([both, both], axis=1)
    total = jnp.zeros((rank, height), F32)
    for week in range(0, weeks, together):
        rows = tile[week : week + together].reshape(together * height, width)
        sums = lax.dot_general(both, rows, (((1,), (1,)), ((), ())), preferred_element_type=F32)
        for part in range(together):
            here = sums[:, part * height : (part + 1) * height]
            total += (here[:rank] + here[rank:]) * spread[week + part]
    return total


def item_term(spread, users, tile):
    weeks, height, width = tile.shape
    width //= 2
    rank = users.shape[0]
    total = jnp.zeros((2 * rank, 2 * width), F32)
    for week in range(0, weeks, 2):
        left = [
            jnp.concatenate(split(spread[part] * users), axis=0) for part in (week, week + 1)
        ]
        total += jnp.dot(
            jnp.concatenate(left, axis=1),
            jnp.concatenate([tile[week], tile[week + 1]], axis=0),
            preferred_element_type=F32,
        )
    half = total[:rank] + total[rank:]
    return half[:, :width] + half[:, width:]


def mode1_kernel(groups, count_ref, users_ref, items_ref, spread, tiles, own, sibling, *refs):
    *messages, even, odd, sums = refs
    height, width = tiles.shape[2], tiles.shape[3] // 2
    me = lax.axis_index("users")
    column = lax.axis_index("items")
    per_device = own.shape[1] // width
    kept = even.shape[2] // height
    sums[...] = jnp.zeros_like(sums)

    def work(slot, carry):
        index = items_ref[0, slot]
        device = index // per_device
        place = columns(index % per_device, width)
        items = jnp.where(device == me, own[:, place], sibling[:, place])
        source = (device // 2) ^ (me // 2)
        here = columns(slot, width)
        for step, message in enumerate(messages):
            items = jnp.where(source == step + 1, message[:, here], items)
        sums[users_ref[0, slot]] += user_term(spread, items, tiles.at[slot])
        return carry

    lax.fori_loop(0, count_ref[0, 0], work, 0)
    for step in range(groups):
        first = (column ^ step) * kept
        for block in range(kept):
            target = (even, odd)[step % 2]
            target[step // 2, :, block * height : (block + 1) * height] = sums[first + block]


def mode2_kernel(count_ref, users_ref, spread, tiles, _, *refs):
    *factors, terms = refs
    height, width = tiles.shape[2], tiles.shape[3] // 2
    column = lax.axis_index("items")
    kept = factors[0].shape[1] // height
    terms[...] = jnp.zeros_like(terms)

    def work(slot, carry):
        block = users_ref[0, slot]
        source = (block // kept) ^ column
        place = columns(block % kept, height)
        users = factors[0][:, place]
        for step in range(1, len(factors)):
            users = jnp.where(source == step, factors[step][:, place], users)
        terms[:, columns(slot, width)] = item_term(spread, users, tiles.at[slot])
        return carry

    lax.fori_loop(0, count_ref[0, 0], work, 0)


def collect_kernel(ids, *refs):
    *terms, own, other = refs
    slots = ids.shape[1]
    width = terms[0].shape[1] // slots
    per_device = own.shape[1] // width
    me = lax.axis_index("users")
    own[...] = jnp.zeros_like(own)
    other[...] = jnp.zeros_like(other)
    for step, term in enumerate(terms):
        for slot in range(slots):
            index = ids[step, slot]
            device = index // per_device
            place = columns(index % per_device, width)
            for owner, target in ((me, own), (me ^ 1, other)):

                @pl.when(device == owner)
                def _():
                    target[:, place] += term[:, slot * width : (slot + 1) * width]


def finish_users_kernel(kept, arrived, total, done):
    total[...] = kept[...] + arrived[...]
    done[...] = jnp.zeros_like(done)


def finish_items_kernel(own, arrived, _, total):
    total[...] = own[...] + arrived[...]


def on_device(sizes, tiles, user_blocks, item_blocks, counts, user_factor, item_factor, week_factor):
    rows, groups = sizes
    chips = rows // 2
    tiles = tiles[0, 0]
    slots, weeks, height, width = tiles.shape
    rank = week_factor.shape[1]
    user_width = user_factor.shape[1]

    def limit(mebibytes):
        return pltpu.CompilerParams(vmem_limit_bytes=mebibytes << 20)

    def cost(times):
        return pl.CostEstimate(
            flops=int(times * 8 * slots * weeks * height * width * rank),
            bytes_accessed=int(times * 4 * slots * weeks * height * width),
            transcendentals=0,
        )

    def across_chips(value, step):
        return lax.ppermute(value, "users", [(i, i ^ (2 * step)) for i in range(rows)])

    def across_cores(value):
        return lax.ppermute(value, "users", [(i, i ^ 1) for i in range(rows)])

    def across_groups(value, step):
        return lax.ppermute(value, "items", [(i, i ^ step) for i in range(groups)])

    def array(*shape, dtype=F32):
        return jax.ShapeDtypeStruct(shape, dtype)

    sibling = across_cores(item_factor)
    asked = [item_blocks[0]] + [across_chips(item_blocks[0], step) for step in range(1, chips)]
    near = jnp.concatenate(asked, axis=0)
    far_users = across_groups(user_factor, groups // 2)
    held = pl.pallas_call(
        hold_kernel,
        out_shape=array(8, 128),
        out_specs=VMEM,
        compiler_params=limit(4),
        cost_estimate=cost(4),
        name="hold",
    )()

    served = pl.pallas_call(
        functools.partial(serve_kernel, chips, width),
        out_shape=[array(rank, slots * width)] * (chips - 1),
        in_specs=[SMEM] + [VMEM] * 2 + [ANY],
        out_specs=[VMEM] * (chips - 1),
        compiler_params=limit(4),
        cost_estimate=cost(1),
        name="serve",
    )(near, item_factor, sibling, held)
    messages = [across_chips(value, step + 1) for step, value in enumerate(served)]

    halves, spread, far_users = pl.pallas_call(
        prepare_kernel,
        out_shape=[
            array(slots, weeks, height, 2 * width, dtype=BF16),
            array(weeks, rank, height),
            array(rank, user_width),
        ],
        in_specs=[SMEM] + [VMEM] * 3 + [ANY],
        out_specs=[VMEM] * 3,
        compiler_params=limit(24),
        name="prepare",
    )(counts, tiles, week_factor, far_users, served[0])
    row_factors = {0: user_factor, groups // 2: far_users}
    step = groups // 4
    while step:
        row_factors |= {at ^ step: across_groups(v, step) for at, v in row_factors.items()}
        step //= 2

    even, odd = pl.pallas_call(
        functools.partial(mode1_kernel, groups),
        out_shape=[array(groups // 2, rank, user_width)] * 2,
        in_specs=[SMEM] * 3 + [VMEM] * (3 + chips),
        out_specs=[VMEM] * 2,
        scratch_shapes=[pltpu.VMEM((groups * user_width // height, rank, height), F32)],
        compiler_params=limit(8),
        cost_estimate=cost(1),
        name="mode1",
    )(
        counts,
        user_blocks[0],
        item_blocks[0],
        spread,
        halves,
        item_factor,
        sibling,
        *messages,
    )
    terms = pl.pallas_call(
        mode2_kernel,
        out_shape=array(rank, slots * width),
        in_specs=[SMEM] * 2 + [VMEM] * 2 + [ANY] + [VMEM] * groups,
        out_specs=VMEM,
        compiler_params=limit(8),
        cost_estimate=cost(2),
        name="mode2",
    )(
        counts,
        user_blocks[0],
        spread,
        halves,
        even,
        *(row_factors[step] for step in range(groups)),
    )
    near_terms = [terms] + [across_chips(terms, step) for step in range(1, chips)]
    own, other = pl.pallas_call(
        collect_kernel,
        out_shape=[array(*item_factor.shape)] * 2,
        in_specs=[SMEM] + [VMEM] * chips,
        out_specs=[VMEM] * 2,
        compiler_params=limit(4),
        name="collect",
    )(near, *near_terms)
    kept, sent, step = even, odd, 1
    while step < groups // 2:
        arrived = across_groups(sent, step)
        kept, sent = kept[0::2] + arrived[0::2], kept[1::2] + arrived[1::2]
        step *= 2
    m_users, done = pl.pallas_call(
        finish_users_kernel,
        out_shape=[array(rank, user_width), array(8, 128)],
        in_specs=[VMEM] * 2,
        out_specs=[VMEM] * 2,
        compiler_params=limit(4),
        cost_estimate=cost(4),
        name="finish_users",
    )(kept[0], across_groups(sent[0], step))
    m_items = pl.pallas_call(
        finish_items_kernel,
        out_shape=array(*item_factor.shape),
        in_specs=[VMEM] * 2 + [ANY],
        out_specs=VMEM,
        compiler_params=limit(4),
        name="finish_items",
    )(own, across_cores(other), done)
    return m_users, m_items


def solution(mesh):
    rows, groups = mesh.shape["users"], mesh.shape["items"]
    assert rows > 1 and rows & (rows - 1) == 0 and groups > 1 and groups & (groups - 1) == 0
    return jax.shard_map(
        functools.partial(on_device, (rows, groups)),
        mesh=mesh,
        in_specs=(
            P("users", "items", None, None, None, None),
            P("users", "items", None),
            P("users", "items", None),
            P("users", "items"),
            P(None, ("users", "items")),
            P(None, ("items", "users")),
            P(),
        ),
        out_specs=(P(None, ("users", "items")), P(None, ("items", "users"))),
        check_vma=False,
    )
```

```python
import functools

import jax
import jax.numpy as jnp
from jax import lax
from jax.experimental import pallas as pl
from jax.experimental.pallas import tpu as pltpu
from jax.sharding import PartitionSpec as P

F32 = jnp.float32
BF16 = jnp.bfloat16
ANY = pl.BlockSpec(memory_space=pl.ANY)
HBM = pl.BlockSpec(memory_space=pltpu.HBM)
SMEM = pl.BlockSpec(memory_space=pltpu.SMEM)
VMEM = pl.BlockSpec(memory_space=pltpu.VMEM)


def columns(block, width):
    return pl.ds(pl.multiple_of(block * width, width), width)


def split(value):
    high = value.astype(BF16)
    return high, (value - high.astype(F32)).astype(BF16)


def hold_kernel(done):
    done[...] = jnp.zeros_like(done)


def prepare_kernel(count_ref, tiles, week_factor, users, _, halves, spread, doubled, users_out):
    weeks, width = tiles.shape[1], tiles.shape[3]
    users_out[...] = users[...]
    doubled[...] = jnp.concatenate([week_factor[...]] * 2, axis=1)
    weeks_t = week_factor[...].T
    for week in range(weeks):
        spread[week] = jnp.broadcast_to(weeks_t[:, week : week + 1], spread.shape[1:])

    def work(slot, carry):
        def one(week, inner):
            high, low = split(tiles[slot, week])
            halves[slot, week, :, :width] = high
            halves[slot, week, :, width:] = low
            return inner

        return lax.fori_loop(0, weeks, one, carry, unroll=8)

    lax.fori_loop(0, count_ref[0, 0], work, 0)


def serve_kernel(chips, width, requests, own, sibling, _, *messages):
    me = lax.axis_index("users")
    per_device = own.shape[1] // width
    for step in range(1, chips):
        for slot in range(requests.shape[1]):
            index = requests[step, slot]
            device = index // per_device
            place = columns(index % per_device, width)
            for owner, source in ((me, own), (me ^ 1, sibling)):

                @pl.when(device == owner)
                def _():
                    messages[step - 1][:, slot * width : (slot + 1) * width] = source[:, place]


def user_term(spread, doubled, items, tile, together=4):
    weeks, height, width = tile.shape
    rank = items.shape[0]
    high, low = split(items)
    flat = jnp.concatenate([high, low], axis=0)
    both = jnp.concatenate([flat, flat], axis=1)
    tall = jnp.concatenate([high.astype(F32), low.astype(F32)], axis=0).T.astype(BF16)
    tall = jnp.concatenate([tall, tall], axis=0)
    total = jnp.zeros((rank, height), F32)
    turned = jnp.zeros((height, 2 * rank), F32)
    for week in range(0, weeks, 2 * together):
        middle = week + together
        rows = tile[week:middle].reshape(together * height, width)
        left = jnp.dot(rows, tall, preferred_element_type=F32)
        rows = tile[middle : middle + together].reshape(together * height, width)
        right = lax.dot_general(both, rows, (((1,), (1,)), ((), ())), preferred_element_type=F32)
        for part in range(together):
            here = slice(part * height, (part + 1) * height)
            turned += left[here] * doubled[week + part, :][None]
            total += (right[:rank, here] + right[rank:, here]) * spread[middle + part]
    turned = turned.T
    return total + turned[:rank] + turned[rank:]


def item_term(spread, users, tile):
    weeks, height, width = tile.shape
    width //= 2
    rank = users.shape[0]
    total = jnp.zeros((2 * rank, 2 * width), F32)
    for week in range(0, weeks, 2):
        left = [
            jnp.concatenate(split(spread[part] * users), axis=0) for part in (week, week + 1)
        ]
        total += jnp.dot(
            jnp.concatenate(left, axis=1),
            jnp.concatenate([tile[week], tile[week + 1]], axis=0),
            preferred_element_type=F32,
        )
    half = total[:rank] + total[rank:]
    return half[:, :width] + half[:, width:]


def mode1_kernel(groups, count_ref, users_ref, items_ref, spread, doubled, tiles, own, sibling, *refs):
    *messages, even, odd, sums = refs
    height, width = tiles.shape[2], tiles.shape[3] // 2
    me = lax.axis_index("users")
    column = lax.axis_index("items")
    per_device = own.shape[1] // width
    kept = even.shape[2] // height
    sums[...] = jnp.zeros_like(sums)

    def work(slot, carry):
        index = items_ref[0, slot]
        device = index // per_device
        place = columns(index % per_device, width)
        items = jnp.where(device == me, own[:, place], sibling[:, place])
        source = (device // 2) ^ (me // 2)
        here = columns(slot, width)
        for step, message in enumerate(messages):
            items = jnp.where(source == step + 1, message[:, here], items)
        sums[users_ref[0, slot]] += user_term(spread, doubled, items, tiles.at[slot])
        return carry

    lax.fori_loop(0, count_ref[0, 0], work, 0)
    for step in range(groups):
        first = (column ^ step) * kept
        for block in range(kept):
            target = (even, odd)[step % 2]
            target[step // 2, :, block * height : (block + 1) * height] = sums[first + block]


def mode2_kernel(count_ref, users_ref, spread, tiles, _, *refs):
    *factors, terms = refs
    height, width = tiles.shape[2], tiles.shape[3] // 2
    column = lax.axis_index("items")
    kept = factors[0].shape[1] // height
    terms[...] = jnp.zeros_like(terms)

    def work(slot, carry):
        block = users_ref[0, slot]
        source = (block // kept) ^ column
        place = columns(block % kept, height)
        users = factors[0][:, place]
        for step in range(1, len(factors)):
            users = jnp.where(source == step, factors[step][:, place], users)
        terms[:, columns(slot, width)] = item_term(spread, users, tiles.at[slot])
        return carry

    lax.fori_loop(0, count_ref[0, 0], work, 0)


def collect_kernel(ids, *refs):
    *terms, own, other = refs
    slots = ids.shape[1]
    width = terms[0].shape[1] // slots
    per_device = own.shape[1] // width
    me = lax.axis_index("users")
    own[...] = jnp.zeros_like(own)
    other[...] = jnp.zeros_like(other)
    for step, term in enumerate(terms):
        for slot in range(slots):
            index = ids[step, slot]
            device = index // per_device
            place = columns(index % per_device, width)
            for owner, target in ((me, own), (me ^ 1, other)):

                @pl.when(device == owner)
                def _():
                    target[:, place] += term[:, slot * width : (slot + 1) * width]


def finish_users_kernel(kept, arrived, total):
    total[...] = kept[...] + arrived[...]


def finish_items_kernel(own, arrived, users, items_out, users_out):
    users_out[...] = users[...]
    items_out[...] = own[...] + arrived[...]


def on_device(sizes, tiles, user_blocks, item_blocks, counts, user_factor, item_factor, week_factor):
    rows, groups = sizes
    chips = rows // 2
    tiles = tiles[0, 0]
    slots, weeks, height, width = tiles.shape
    rank = week_factor.shape[1]
    user_width = user_factor.shape[1]

    def limit(mebibytes):
        return pltpu.CompilerParams(vmem_limit_bytes=mebibytes << 20)

    def cost(times):
        return pl.CostEstimate(
            flops=int(times * 8 * slots * weeks * height * width * rank),
            bytes_accessed=int(times * 4 * slots * weeks * height * width),
            transcendentals=0,
        )

    def across_chips(value, step):
        return lax.ppermute(value, "users", [(i, i ^ (2 * step)) for i in range(rows)])

    def across_cores(value):
        return lax.ppermute(value, "users", [(i, i ^ 1) for i in range(rows)])

    def across_groups(value, step):
        return lax.ppermute(value, "items", [(i, i ^ step) for i in range(groups)])

    def array(*shape, dtype=F32):
        return jax.ShapeDtypeStruct(shape, dtype)

    sibling = across_cores(item_factor)
    asked = [item_blocks[0]] + [across_chips(item_blocks[0], step) for step in range(1, chips)]
    near = jnp.concatenate(asked, axis=0)
    far_users = across_groups(user_factor, groups // 2)
    held = pl.pallas_call(
        hold_kernel,
        out_shape=array(8, 128),
        out_specs=VMEM,
        compiler_params=limit(4),
        cost_estimate=cost(4),
        name="hold",
    )()

    served = pl.pallas_call(
        functools.partial(serve_kernel, chips, width),
        out_shape=[array(rank, slots * width)] * (chips - 1),
        in_specs=[SMEM] + [VMEM] * 2 + [ANY],
        out_specs=[VMEM] * (chips - 1),
        compiler_params=limit(4),
        cost_estimate=cost(1),
        name="serve",
    )(near, item_factor, sibling, held)
    messages = [across_chips(value, step + 1) for step, value in enumerate(served)]

    halves, spread, doubled, far_users = pl.pallas_call(
        prepare_kernel,
        out_shape=[
            array(slots, weeks, height, 2 * width, dtype=BF16),
            array(weeks, rank, height),
            array(weeks, 2 * rank),
            array(rank, user_width),
        ],
        in_specs=[SMEM] + [VMEM] * 3 + [ANY],
        out_specs=[VMEM] * 4,
        compiler_params=limit(24),
        name="prepare",
    )(counts, tiles, week_factor, far_users, served[0])
    row_factors = {0: user_factor, groups // 2: far_users}
    step = groups // 4
    while step:
        row_factors |= {at ^ step: across_groups(v, step) for at, v in row_factors.items()}
        step //= 2

    even, odd = pl.pallas_call(
        functools.partial(mode1_kernel, groups),
        out_shape=[array(groups // 2, rank, user_width)] * 2,
        in_specs=[SMEM] * 3 + [VMEM] * (4 + chips),
        out_specs=[VMEM] * 2,
        scratch_shapes=[pltpu.VMEM((groups * user_width // height, rank, height), F32)],
        compiler_params=limit(8),
        cost_estimate=cost(1),
        name="mode1",
    )(
        counts,
        user_blocks[0],
        item_blocks[0],
        spread,
        doubled,
        halves,
        item_factor,
        sibling,
        *messages,
    )
    terms = pl.pallas_call(
        mode2_kernel,
        out_shape=array(rank, slots * width),
        in_specs=[SMEM] * 2 + [VMEM] * 2 + [ANY] + [VMEM] * groups,
        out_specs=VMEM,
        compiler_params=limit(8),
        cost_estimate=cost(2),
        name="mode2",
    )(
        counts,
        user_blocks[0],
        spread,
        halves,
        even,
        *(row_factors[step] for step in range(groups)),
    )
    near_terms = [terms] + [across_chips(terms, step) for step in range(1, chips)]
    own, other = pl.pallas_call(
        collect_kernel,
        out_shape=[array(*item_factor.shape)] * 2,
        in_specs=[SMEM] + [VMEM] * chips,
        out_specs=[VMEM] * 2,
        compiler_params=limit(4),
        name="collect",
    )(near, *near_terms)
    kept, sent, step = even, odd, 1
    while step < groups // 2:
        arrived = across_groups(sent, step)
        kept, sent = kept[0::2] + arrived[0::2], kept[1::2] + arrived[1::2]
        step *= 2
    users = pl.pallas_call(
        finish_users_kernel,
        out_shape=array(rank, user_width),
        in_specs=[VMEM] * 2,
        out_specs=VMEM,
        compiler_params=limit(4),
        cost_estimate=cost(4),
        name="finish_users",
    )(kept[0], across_groups(sent[0], step))
    m_items, m_users = pl.pallas_call(
        finish_items_kernel,
        out_shape=[array(*item_factor.shape), array(rank, user_width)],
        in_specs=[VMEM] * 3,
        out_specs=[VMEM] * 2,
        compiler_params=limit(4),
        name="finish_items",
    )(own, across_cores(other), users)
    return m_users, m_items


def solution(mesh):
    rows, groups = mesh.shape["users"], mesh.shape["items"]
    assert rows > 1 and rows & (rows - 1) == 0 and groups > 1 and groups & (groups - 1) == 0
    return jax.shard_map(
        functools.partial(on_device, (rows, groups)),
        mesh=mesh,
        in_specs=(
            P("users", "items", None, None, None, None),
            P("users", "items", None),
            P("users", "items", None),
            P("users", "items"),
            P(None, ("users", "items")),
            P(None, ("items", "users")),
            P(),
        ),
        out_specs=(P(None, ("users", "items")), P(None, ("items", "users"))),
        check_vma=False,
    )
```

```python
import functools

import jax
import jax.numpy as jnp
from jax import lax
from jax.experimental import pallas as pl
from jax.experimental.pallas import tpu as pltpu
from jax.sharding import PartitionSpec as P

F32 = jnp.float32
BF16 = jnp.bfloat16
ANY = pl.BlockSpec(memory_space=pl.ANY)
HBM = pl.BlockSpec(memory_space=pltpu.HBM)
SMEM = pl.BlockSpec(memory_space=pltpu.SMEM)
VMEM = pl.BlockSpec(memory_space=pltpu.VMEM)


def columns(block, width):
    return pl.ds(pl.multiple_of(block * width, width), width)


def split(value):
    high = value.astype(BF16)
    return high, (value - high.astype(F32)).astype(BF16)


def hold_kernel(done):
    done[...] = jnp.zeros_like(done)


def prepare_kernel(count_ref, tiles, week_factor, users, _, halves, spread, users_out):
    weeks, width = tiles.shape[1], tiles.shape[3]
    users_out[...] = users[...]
    weeks_t = week_factor[...].T
    for week in range(weeks):
        spread[week] = jnp.broadcast_to(weeks_t[:, week : week + 1], spread.shape[1:])

    def work(slot, carry):
        def one(week, inner):
            high, low = split(tiles[slot, week])
            halves[slot, week, :, :width] = high
            halves[slot, week, :, width:] = low
            return inner

        return lax.fori_loop(0, weeks, one, carry, unroll=8)

    lax.fori_loop(0, count_ref[0, 0], work, 0)


def serve_kernel(chips, width, requests, own, sibling, _, *messages):
    me = lax.axis_index("users")
    per_device = own.shape[1] // width
    for step in range(1, chips):
        for slot in range(requests.shape[1]):
            index = requests[step, slot]
            device = index // per_device
            place = columns(index % per_device, width)
            for owner, source in ((me, own), (me ^ 1, sibling)):

                @pl.when(device == owner)
                def _():
                    messages[step - 1][:, slot * width : (slot + 1) * width] = source[:, place]


def quarters(sums, size):
    total = pltpu.matmul_pop(sums[0])
    for other in sums[1:]:
        total += pltpu.matmul_pop(other)
    half = total[: total.shape[0] // 2] + total[total.shape[0] // 2 :]
    return half[:, :size] + half[:, size:]


def multiply(sums, at, left, right, transpose):
    unit, stage = at % len(sums), at // len(sums) % 2
    pltpu.matmul_push_rhs(right, stage, unit, transpose=transpose)
    pltpu.matmul_acc_lhs(sums[unit], left, load_staged_rhs=stage)


def user_term(spread, items, tile, sums):
    weeks, height, width = tile.shape
    width //= 2
    for at in range(weeks // 2):
        left, right = [], []
        for part in (2 * at, 2 * at + 1):
            left.append(jnp.concatenate(split(spread[part] * items), axis=0))
            right.append(jnp.concatenate([tile[part, :, :width], tile[part, :, width:]], axis=0))
        left, right = jnp.concatenate(left, axis=1), jnp.concatenate(right, axis=1)
        multiply(sums, at, left, right, True)
    return quarters(sums, height)


def item_term(spread, users, tile, sums):
    weeks, height, width = tile.shape
    for at in range(weeks // 2):
        left = [
            jnp.concatenate(split(spread[part] * users), axis=0) for part in (2 * at, 2 * at + 1)
        ]
        right = tile[2 * at : 2 * at + 2].reshape(2 * height, width)
        multiply(sums, at, jnp.concatenate(left, axis=1), right, False)
    return quarters(sums, width // 2)


def mode1_kernel(groups, units, count_ref, users_ref, items_ref, spread, tiles, own, sibling, *refs):
    *messages, even, odd, sums = refs
    height, width = tiles.shape[2], tiles.shape[3] // 2
    me = lax.axis_index("users")
    column = lax.axis_index("items")
    per_device = own.shape[1] // width
    kept = even.shape[2] // height
    sums[...] = jnp.zeros_like(sums)

    def work(slot, carry):
        index = items_ref[0, slot]
        device = index // per_device
        place = columns(index % per_device, width)
        items = jnp.where(device == me, own[:, place], sibling[:, place])
        source = (device // 2) ^ (me // 2)
        here = columns(slot, width)
        for step, message in enumerate(messages):
            items = jnp.where(source == step + 1, message[:, here], items)
        sums[users_ref[0, slot]] += pl.run_scoped(
            lambda *held: user_term(spread, items, tiles.at[slot], held), *units
        )
        return carry

    lax.fori_loop(0, count_ref[0, 0], work, 0)
    for step in range(groups):
        first = (column ^ step) * kept
        for block in range(kept):
            target = (even, odd)[step % 2]
            target[step // 2, :, block * height : (block + 1) * height] = sums[first + block]


def mode2_kernel(units, count_ref, users_ref, spread, tiles, _, *refs):
    *factors, terms = refs
    height, width = tiles.shape[2], tiles.shape[3] // 2
    column = lax.axis_index("items")
    kept = factors[0].shape[1] // height
    terms[...] = jnp.zeros_like(terms)

    def work(slot, carry):
        block = users_ref[0, slot]
        source = (block // kept) ^ column
        place = columns(block % kept, height)
        users = factors[0][:, place]
        for step in range(1, len(factors)):
            users = jnp.where(source == step, factors[step][:, place], users)
        terms[:, columns(slot, width)] = pl.run_scoped(
            lambda *held: item_term(spread, users, tiles.at[slot], held), *units
        )
        return carry

    lax.fori_loop(0, count_ref[0, 0], work, 0)


def collect_kernel(ids, *refs):
    *terms, own, other = refs
    slots = ids.shape[1]
    width = terms[0].shape[1] // slots
    per_device = own.shape[1] // width
    me = lax.axis_index("users")
    own[...] = jnp.zeros_like(own)
    other[...] = jnp.zeros_like(other)
    for step, term in enumerate(terms):
        for slot in range(slots):
            index = ids[step, slot]
            device = index // per_device
            place = columns(index % per_device, width)
            for owner, target in ((me, own), (me ^ 1, other)):

                @pl.when(device == owner)
                def _():
                    target[:, place] += term[:, slot * width : (slot + 1) * width]


def finish_users_kernel(kept, arrived, total):
    total[...] = kept[...] + arrived[...]


def finish_items_kernel(own, arrived, users, items_out, users_out):
    users_out[...] = users[...]
    items_out[...] = own[...] + arrived[...]


def on_device(mesh, tiles, user_blocks, item_blocks, counts, user_factor, item_factor, week_factor):
    rows, groups = mesh.shape["users"], mesh.shape["items"]
    chips = rows // 2
    tiles = tiles[0, 0]
    slots, weeks, height, width = tiles.shape
    rank = week_factor.shape[1]
    user_width = user_factor.shape[1]

    def limit(mebibytes):
        return pltpu.CompilerParams(vmem_limit_bytes=mebibytes << 20)

    def cost(times):
        return pl.CostEstimate(
            flops=int(times * 8 * slots * weeks * height * width * rank),
            bytes_accessed=int(times * 4 * slots * weeks * height * width),
            transcendentals=0,
        )

    with jax.sharding.use_abstract_mesh(mesh.abstract_mesh):
        units = [pltpu.ACC(unit)((2 * rank, 2 * width), F32) for unit in range(2)]

    def across_chips(value, step):
        return lax.ppermute(value, "users", [(i, i ^ (2 * step)) for i in range(rows)])

    def across_cores(value):
        return lax.ppermute(value, "users", [(i, i ^ 1) for i in range(rows)])

    def across_groups(value, step):
        return lax.ppermute(value, "items", [(i, i ^ step) for i in range(groups)])

    def array(*shape, dtype=F32):
        return jax.ShapeDtypeStruct(shape, dtype)

    sibling = across_cores(item_factor)
    asked = [item_blocks[0]] + [across_chips(item_blocks[0], step) for step in range(1, chips)]
    near = jnp.concatenate(asked, axis=0)
    far_users = across_groups(user_factor, groups // 2)
    held = pl.pallas_call(
        hold_kernel,
        out_shape=array(8, 128),
        out_specs=VMEM,
        compiler_params=limit(4),
        cost_estimate=cost(4),
        name="hold",
    )()

    served = pl.pallas_call(
        functools.partial(serve_kernel, chips, width),
        out_shape=[array(rank, slots * width)] * (chips - 1),
        in_specs=[SMEM] + [VMEM] * 2 + [ANY],
        out_specs=[VMEM] * (chips - 1),
        compiler_params=limit(4),
        cost_estimate=cost(1),
        name="serve",
    )(near, item_factor, sibling, held)
    messages = [across_chips(value, step + 1) for step, value in enumerate(served)]

    halves, spread, far_users = pl.pallas_call(
        prepare_kernel,
        out_shape=[
            array(slots, weeks, height, 2 * width, dtype=BF16),
            array(weeks, rank, height),
            array(rank, user_width),
        ],
        in_specs=[SMEM] + [VMEM] * 3 + [ANY],
        out_specs=[VMEM] * 3,
        compiler_params=limit(24),
        name="prepare",
    )(counts, tiles, week_factor, far_users, served[0])
    row_factors = {0: user_factor, groups // 2: far_users}
    step = groups // 4
    while step:
        row_factors |= {at ^ step: across_groups(v, step) for at, v in row_factors.items()}
        step //= 2

    even, odd = pl.pallas_call(
        functools.partial(mode1_kernel, groups, units),
        out_shape=[array(groups // 2, rank, user_width)] * 2,
        in_specs=[SMEM] * 3 + [VMEM] * (3 + chips),
        out_specs=[VMEM] * 2,
        scratch_shapes=[pltpu.VMEM((groups * user_width // height, rank, height), F32)],
        compiler_params=limit(8),
        cost_estimate=cost(1),
        name="mode1",
    )(
        counts,
        user_blocks[0],
        item_blocks[0],
        spread,
        halves,
        item_factor,
        sibling,
        *messages,
    )
    terms = pl.pallas_call(
        functools.partial(mode2_kernel, units),
        out_shape=array(rank, slots * width),
        in_specs=[SMEM] * 2 + [VMEM] * 2 + [ANY] + [VMEM] * groups,
        out_specs=VMEM,
        compiler_params=limit(8),
        cost_estimate=cost(2),
        name="mode2",
    )(
        counts,
        user_blocks[0],
        spread,
        halves,
        even,
        *(row_factors[step] for step in range(groups)),
    )
    near_terms = [terms] + [across_chips(terms, step) for step in range(1, chips)]
    own, other = pl.pallas_call(
        collect_kernel,
        out_shape=[array(*item_factor.shape)] * 2,
        in_specs=[SMEM] + [VMEM] * chips,
        out_specs=[VMEM] * 2,
        compiler_params=limit(4),
        name="collect",
    )(near, *near_terms)
    kept, sent, step = even, odd, 1
    while step < groups // 2:
        arrived = across_groups(sent, step)
        kept, sent = kept[0::2] + arrived[0::2], kept[1::2] + arrived[1::2]
        step *= 2
    users = pl.pallas_call(
        finish_users_kernel,
        out_shape=array(rank, user_width),
        in_specs=[VMEM] * 2,
        out_specs=VMEM,
        compiler_params=limit(4),
        cost_estimate=cost(4),
        name="finish_users",
    )(kept[0], across_groups(sent[0], step))
    m_items, m_users = pl.pallas_call(
        finish_items_kernel,
        out_shape=[array(*item_factor.shape), array(rank, user_width)],
        in_specs=[VMEM] * 3,
        out_specs=[VMEM] * 2,
        compiler_params=limit(4),
        name="finish_items",
    )(own, across_cores(other), users)
    return m_users, m_items


def solution(mesh):
    rows, groups = mesh.shape["users"], mesh.shape["items"]
    assert rows > 1 and rows & (rows - 1) == 0 and groups > 1 and groups & (groups - 1) == 0
    return jax.shard_map(
        functools.partial(on_device, mesh),
        mesh=mesh,
        in_specs=(
            P("users", "items", None, None, None, None),
            P("users", "items", None),
            P("users", "items", None),
            P("users", "items"),
            P(None, ("users", "items")),
            P(None, ("items", "users")),
            P(),
        ),
        out_specs=(P(None, ("users", "items")), P(None, ("items", "users"))),
        check_vma=False,
    )
```

```python
import functools

import jax
import jax.numpy as jnp
from jax import lax
from jax.experimental import pallas as pl
from jax.experimental.pallas import tpu as pltpu
from jax.sharding import PartitionSpec as P

F32 = jnp.float32
BF16 = jnp.bfloat16
ANY = pl.BlockSpec(memory_space=pl.ANY)
HBM = pl.BlockSpec(memory_space=pltpu.HBM)
SMEM = pl.BlockSpec(memory_space=pltpu.SMEM)
VMEM = pl.BlockSpec(memory_space=pltpu.VMEM)


def columns(block, width):
    return pl.ds(pl.multiple_of(block * width, width), width)


def split(value):
    high = value.astype(BF16)
    return high, (value - high.astype(F32)).astype(BF16)


def hold_kernel(done):
    done[...] = jnp.zeros_like(done)


def prepare_kernel(count_ref, tiles, week_factor, users, _, halves, spread, doubled, users_out):
    weeks, width = tiles.shape[1], tiles.shape[3]
    users_out[...] = users[...]
    doubled[...] = jnp.concatenate([week_factor[...]] * 2, axis=1)
    weeks_t = week_factor[...].T
    for week in range(weeks):
        spread[week] = jnp.broadcast_to(weeks_t[:, week : week + 1], spread.shape[1:])

    def work(slot, carry):
        def one(week, inner):
            high, low = split(tiles[slot, week])
            halves[slot, week, :, :width] = high
            halves[slot, week, :, width:] = low
            return inner

        return lax.fori_loop(0, weeks, one, carry, unroll=8)

    lax.fori_loop(0, count_ref[0, 0], work, 0)


def serve_kernel(chips, width, requests, own, sibling, _, *messages):
    me = lax.axis_index("users")
    per_device = own.shape[1] // width
    for step in range(1, chips):
        for slot in range(requests.shape[1]):
            index = requests[step, slot]
            device = index // per_device
            place = columns(index % per_device, width)
            for owner, source in ((me, own), (me ^ 1, sibling)):

                @pl.when(device == owner)
                def _():
                    messages[step - 1][:, slot * width : (slot + 1) * width] = source[:, place]


def user_term(doubled, items, tile, sums):
    weeks, height, width = tile.shape
    rank = items.shape[0]
    high, low = split(items)
    tall = jnp.concatenate([high.astype(F32), low.astype(F32)], axis=0).T.astype(BF16)
    wide = jnp.concatenate([tall, jnp.zeros((width // 2, width - 2 * rank), BF16)], axis=1)
    wide = jnp.concatenate([wide, wide], axis=0)
    units = len(sums) // 2
    together = sums[0].shape[0] // height
    total = jnp.zeros((height, 2 * rank), F32)
    for unit in range(units):
        pltpu.matmul_push_rhs(wide, 0, unit)

    def begin(at):
        rows = tile[at * together : (at + 1) * together].reshape(together * height, width)
        first = {"load_staged_rhs": 0} if at < units else {}
        pltpu.matmul_acc_lhs(sums[at % len(sums)], rows, **first)

    for at in range(units):
        begin(at)
    for at in range(weeks // together):
        if at + units < weeks // together:
            begin(at + units)
        done = pltpu.matmul_pop(sums[at % len(sums)])[:, : 2 * rank]
        for part in range(together):
            here = done[part * height : (part + 1) * height]
            total += here * doubled[at * together + part, :][None]
    total = total.T
    return total[:rank] + total[rank:]


def item_term(spread, users, tile):
    weeks, height, width = tile.shape
    width //= 2
    rank = users.shape[0]
    total = jnp.zeros((2 * rank, 2 * width), F32)
    for week in range(0, weeks, 2):
        left = [
            jnp.concatenate(split(spread[part] * users), axis=0) for part in (week, week + 1)
        ]
        total += jnp.dot(
            jnp.concatenate(left, axis=1),
            jnp.concatenate([tile[week], tile[week + 1]], axis=0),
            preferred_element_type=F32,
        )
    half = total[:rank] + total[rank:]
    return half[:, :width] + half[:, width:]


def mode1_kernel(groups, units, count_ref, users_ref, items_ref, doubled, tiles, own, sibling, *refs):
    *messages, even, odd, sums = refs
    height, width = tiles.shape[2], tiles.shape[3] // 2
    me = lax.axis_index("users")
    column = lax.axis_index("items")
    per_device = own.shape[1] // width
    kept = even.shape[2] // height
    sums[...] = jnp.zeros_like(sums)

    def work(slot, carry):
        index = items_ref[0, slot]
        device = index // per_device
        place = columns(index % per_device, width)
        items = jnp.where(device == me, own[:, place], sibling[:, place])
        source = (device // 2) ^ (me // 2)
        here = columns(slot, width)
        for step, message in enumerate(messages):
            items = jnp.where(source == step + 1, message[:, here], items)
        sums[users_ref[0, slot]] += pl.run_scoped(
            lambda *held: user_term(doubled, items, tiles.at[slot], held), *units
        )
        return carry

    lax.fori_loop(0, count_ref[0, 0], work, 0)
    for step in range(groups):
        first = (column ^ step) * kept
        for block in range(kept):
            target = (even, odd)[step % 2]
            target[step // 2, :, block * height : (block + 1) * height] = sums[first + block]


def mode2_kernel(count_ref, users_ref, spread, tiles, _, *refs):
    *factors, terms = refs
    height, width = tiles.shape[2], tiles.shape[3] // 2
    column = lax.axis_index("items")
    kept = factors[0].shape[1] // height
    terms[...] = jnp.zeros_like(terms)

    def work(slot, carry):
        block = users_ref[0, slot]
        source = (block // kept) ^ column
        place = columns(block % kept, height)
        users = factors[0][:, place]
        for step in range(1, len(factors)):
            users = jnp.where(source == step, factors[step][:, place], users)
        terms[:, columns(slot, width)] = item_term(spread, users, tiles.at[slot])
        return carry

    lax.fori_loop(0, count_ref[0, 0], work, 0)


def collect_kernel(ids, *refs):
    *terms, own, other = refs
    slots = ids.shape[1]
    width = terms[0].shape[1] // slots
    per_device = own.shape[1] // width
    me = lax.axis_index("users")
    own[...] = jnp.zeros_like(own)
    other[...] = jnp.zeros_like(other)
    for step, term in enumerate(terms):
        for slot in range(slots):
            index = ids[step, slot]
            device = index // per_device
            place = columns(index % per_device, width)
            for owner, target in ((me, own), (me ^ 1, other)):

                @pl.when(device == owner)
                def _():
                    target[:, place] += term[:, slot * width : (slot + 1) * width]


def finish_users_kernel(kept, arrived, total):
    total[...] = kept[...] + arrived[...]


def finish_items_kernel(own, arrived, users, items_out, users_out):
    users_out[...] = users[...]
    items_out[...] = own[...] + arrived[...]


def on_device(mesh, tiles, user_blocks, item_blocks, counts, user_factor, item_factor, week_factor):
    rows, groups = mesh.shape["users"], mesh.shape["items"]
    chips = rows // 2
    tiles = tiles[0, 0]
    slots, weeks, height, width = tiles.shape
    rank = week_factor.shape[1]
    user_width = user_factor.shape[1]

    def limit(mebibytes):
        return pltpu.CompilerParams(vmem_limit_bytes=mebibytes << 20)

    def cost(times):
        return pl.CostEstimate(
            flops=int(times * 8 * slots * weeks * height * width * rank),
            bytes_accessed=int(times * 4 * slots * weeks * height * width),
            transcendentals=0,
        )

    with jax.sharding.use_abstract_mesh(mesh.abstract_mesh):
        units = [pltpu.ACC(unit % 2)((2 * height, 2 * width), F32) for unit in range(4)]

    def across_chips(value, step):
        return lax.ppermute(value, "users", [(i, i ^ (2 * step)) for i in range(rows)])

    def across_cores(value):
        return lax.ppermute(value, "users", [(i, i ^ 1) for i in range(rows)])

    def across_groups(value, step):
        return lax.ppermute(value, "items", [(i, i ^ step) for i in range(groups)])

    def array(*shape, dtype=F32):
        return jax.ShapeDtypeStruct(shape, dtype)

    sibling = across_cores(item_factor)
    asked = [item_blocks[0]] + [across_chips(item_blocks[0], step) for step in range(1, chips)]
    near = jnp.concatenate(asked, axis=0)
    far_users = across_groups(user_factor, groups // 2)
    held = pl.pallas_call(
        hold_kernel,
        out_shape=array(8, 128),
        out_specs=VMEM,
        compiler_params=limit(4),
        cost_estimate=cost(4),
        name="hold",
    )()

    served = pl.pallas_call(
        functools.partial(serve_kernel, chips, width),
        out_shape=[array(rank, slots * width)] * (chips - 1),
        in_specs=[SMEM] + [VMEM] * 2 + [ANY],
        out_specs=[VMEM] * (chips - 1),
        compiler_params=limit(4),
        cost_estimate=cost(1),
        name="serve",
    )(near, item_factor, sibling, held)
    messages = [across_chips(value, step + 1) for step, value in enumerate(served)]

    halves, spread, doubled, far_users = pl.pallas_call(
        prepare_kernel,
        out_shape=[
            array(slots, weeks, height, 2 * width, dtype=BF16),
            array(weeks, rank, height),
            array(weeks, 2 * rank),
            array(rank, user_width),
        ],
        in_specs=[SMEM] + [VMEM] * 3 + [ANY],
        out_specs=[VMEM] * 4,
        compiler_params=limit(24),
        name="prepare",
    )(counts, tiles, week_factor, far_users, served[0])
    row_factors = {0: user_factor, groups // 2: far_users}
    step = groups // 4
    while step:
        row_factors |= {at ^ step: across_groups(v, step) for at, v in row_factors.items()}
        step //= 2

    even, odd = pl.pallas_call(
        functools.partial(mode1_kernel, groups, units),
        out_shape=[array(groups // 2, rank, user_width)] * 2,
        in_specs=[SMEM] * 3 + [VMEM] * (3 + chips),
        out_specs=[VMEM] * 2,
        scratch_shapes=[pltpu.VMEM((groups * user_width // height, rank, height), F32)],
        compiler_params=limit(8),
        cost_estimate=cost(1),
        name="mode1",
    )(
        counts,
        user_blocks[0],
        item_blocks[0],
        doubled,
        halves,
        item_factor,
        sibling,
        *messages,
    )
    terms = pl.pallas_call(
        mode2_kernel,
        out_shape=array(rank, slots * width),
        in_specs=[SMEM] * 2 + [VMEM] * 2 + [ANY] + [VMEM] * groups,
        out_specs=VMEM,
        compiler_params=limit(8),
        cost_estimate=cost(2),
        name="mode2",
    )(
        counts,
        user_blocks[0],
        spread,
        halves,
        even,
        *(row_factors[step] for step in range(groups)),
    )
    near_terms = [terms] + [across_chips(terms, step) for step in range(1, chips)]
    own, other = pl.pallas_call(
        collect_kernel,
        out_shape=[array(*item_factor.shape)] * 2,
        in_specs=[SMEM] + [VMEM] * chips,
        out_specs=[VMEM] * 2,
        compiler_params=limit(4),
        name="collect",
    )(near, *near_terms)
    kept, sent, step = even, odd, 1
    while step < groups // 2:
        arrived = across_groups(sent, step)
        kept, sent = kept[0::2] + arrived[0::2], kept[1::2] + arrived[1::2]
        step *= 2
    users = pl.pallas_call(
        finish_users_kernel,
        out_shape=array(rank, user_width),
        in_specs=[VMEM] * 2,
        out_specs=VMEM,
        compiler_params=limit(4),
        cost_estimate=cost(4),
        name="finish_users",
    )(kept[0], across_groups(sent[0], step))
    m_items, m_users = pl.pallas_call(
        finish_items_kernel,
        out_shape=[array(*item_factor.shape), array(rank, user_width)],
        in_specs=[VMEM] * 3,
        out_specs=[VMEM] * 2,
        compiler_params=limit(4),
        name="finish_items",
    )(own, across_cores(other), users)
    return m_users, m_items


def solution(mesh):
    rows, groups = mesh.shape["users"], mesh.shape["items"]
    assert rows > 1 and rows & (rows - 1) == 0 and groups > 1 and groups & (groups - 1) == 0
    return jax.shard_map(
        functools.partial(on_device, mesh),
        mesh=mesh,
        in_specs=(
            P("users", "items", None, None, None, None),
            P("users", "items", None),
            P("users", "items", None),
            P("users", "items"),
            P(None, ("users", "items")),
            P(None, ("items", "users")),
            P(),
        ),
        out_specs=(P(None, ("users", "items")), P(None, ("items", "users"))),
        check_vma=False,
    )
```

```python
import functools

import jax
import jax.numpy as jnp
from jax import lax
from jax.experimental import pallas as pl
from jax.experimental.pallas import tpu as pltpu
from jax.sharding import PartitionSpec as P

F32 = jnp.float32
BF16 = jnp.bfloat16
ANY = pl.BlockSpec(memory_space=pl.ANY)
HBM = pl.BlockSpec(memory_space=pltpu.HBM)
SMEM = pl.BlockSpec(memory_space=pltpu.SMEM)
VMEM = pl.BlockSpec(memory_space=pltpu.VMEM)


def columns(block, width):
    return pl.ds(pl.multiple_of(block * width, width), width)


def split(value):
    high = value.astype(BF16)
    return high, (value - high.astype(F32)).astype(BF16)


def hold_kernel(_, done):
    done[...] = jnp.zeros_like(done)


def prepare_kernel(count_ref, tiles, week_factor, users, _, halves, spread, users_out):
    weeks, width = tiles.shape[1], tiles.shape[3]
    users_out[...] = users[...]
    weeks_t = week_factor[...].T
    for week in range(weeks):
        spread[week] = jnp.broadcast_to(weeks_t[:, week : week + 1], spread.shape[1:])

    def work(slot, carry):
        def one(week, inner):
            high, low = split(tiles[slot, week])
            halves[slot, week, :, :width] = high
            halves[slot, week, :, width:] = low
            return inner

        return lax.fori_loop(0, weeks, one, carry, unroll=8)

    lax.fori_loop(0, count_ref[0, 0], work, 0)


def serve_kernel(chips, width, requests, own, sibling, _, *messages):
    me = lax.axis_index("users")
    per_device = own.shape[1] // width
    for step in range(1, chips):
        for slot in range(requests.shape[1]):
            index = requests[step, slot]
            device = index // per_device
            place = columns(index % per_device, width)
            for owner, source in ((me, own), (me ^ 1, sibling)):

                @pl.when(device == owner)
                def _():
                    messages[step - 1][:, slot * width : (slot + 1) * width] = source[:, place]


def user_term(spread, items, tile, together=8):
    weeks, height, width = tile.shape
    rank = items.shape[0]
    both = jnp.concatenate(split(items), axis=0)
    both = jnp.concatenate([both, both], axis=1)
    total = jnp.zeros((rank, height), F32)
    for week in range(0, weeks, together):
        rows = tile[week : week + together].reshape(together * height, width)
        sums = lax.dot_general(both, rows, (((1,), (1,)), ((), ())), preferred_element_type=F32)
        for part in range(together):
            here = sums[:, part * height : (part + 1) * height]
            total += (here[:rank] + here[rank:]) * spread[week + part]
    return total


def item_term(spread, users, tile):
    weeks, height, width = tile.shape
    width //= 2
    rank = users.shape[0]
    total = jnp.zeros((2 * rank, 2 * width), F32)
    for week in range(0, weeks, 2):
        left = [
            jnp.concatenate(split(spread[part] * users), axis=0) for part in (week, week + 1)
        ]
        total += jnp.dot(
            jnp.concatenate(left, axis=1),
            jnp.concatenate([tile[week], tile[week + 1]], axis=0),
            preferred_element_type=F32,
        )
    half = total[:rank] + total[rank:]
    return half[:, :width] + half[:, width:]


def mode1_kernel(groups, count_ref, users_ref, items_ref, spread, tiles, own, sibling, *refs):
    *messages, even, odd, sums = refs
    height, width = tiles.shape[2], tiles.shape[3] // 2
    me = lax.axis_index("users")
    column = lax.axis_index("items")
    per_device = own.shape[1] // width
    kept = even.shape[2] // height
    sums[...] = jnp.zeros_like(sums)

    def work(slot, carry):
        index = items_ref[0, slot]
        device = index // per_device
        place = columns(index % per_device, width)
        items = jnp.where(device == me, own[:, place], sibling[:, place])
        source = (device // 2) ^ (me // 2)
        here = columns(slot, width)
        for step, message in enumerate(messages):
            items = jnp.where(source == step + 1, message[:, here], items)
        sums[users_ref[0, slot]] += user_term(spread, items, tiles.at[slot])
        return carry

    lax.fori_loop(0, count_ref[0, 0], work, 0)
    for step in range(groups):
        first = (column ^ step) * kept
        for block in range(kept):
            target = (even, odd)[step % 2]
            target[step // 2, :, block * height : (block + 1) * height] = sums[first + block]


def mode2_kernel(count_ref, users_ref, spread, tiles, _, *refs):
    *factors, terms = refs
    height, width = tiles.shape[2], tiles.shape[3] // 2
    column = lax.axis_index("items")
    kept = factors[0].shape[1] // height
    terms[...] = jnp.zeros_like(terms)

    def work(slot, carry):
        block = users_ref[0, slot]
        source = (block // kept) ^ column
        place = columns(block % kept, height)
        users = factors[0][:, place]
        for step in range(1, len(factors)):
            users = jnp.where(source == step, factors[step][:, place], users)
        terms[:, columns(slot, width)] = item_term(spread, users, tiles.at[slot])
        return carry

    lax.fori_loop(0, count_ref[0, 0], work, 0)


def collect_kernel(ids, *refs):
    *terms, own, other = refs
    slots = ids.shape[1]
    width = terms[0].shape[1] // slots
    per_device = own.shape[1] // width
    me = lax.axis_index("users")
    own[...] = jnp.zeros_like(own)
    other[...] = jnp.zeros_like(other)
    for step, term in enumerate(terms):
        for slot in range(slots):
            index = ids[step, slot]
            device = index // per_device
            place = columns(index % per_device, width)
            for owner, target in ((me, own), (me ^ 1, other)):

                @pl.when(device == owner)
                def _():
                    target[:, place] += term[:, slot * width : (slot + 1) * width]


def finish_users_kernel(kept, arrived, total):
    total[...] = kept[...] + arrived[...]


def finish_items_kernel(own, arrived, users, items_out, users_out):
    users_out[...] = users[...]
    items_out[...] = own[...] + arrived[...]


def on_device(sizes, tiles, user_blocks, item_blocks, counts, user_factor, item_factor, week_factor):
    rows, groups = sizes
    chips = rows // 2
    tiles = tiles[0, 0]
    slots, weeks, height, width = tiles.shape
    rank = week_factor.shape[1]
    user_width = user_factor.shape[1]

    def limit(mebibytes):
        return pltpu.CompilerParams(vmem_limit_bytes=mebibytes << 20)

    def cost(times):
        return pl.CostEstimate(
            flops=int(times * 8 * slots * weeks * height * width * rank),
            bytes_accessed=int(times * 4 * slots * weeks * height * width),
            transcendentals=0,
        )

    def across_chips(value, step):
        return lax.ppermute(value, "users", [(i, i ^ (2 * step)) for i in range(rows)])

    def across_cores(value):
        return lax.ppermute(value, "users", [(i, i ^ 1) for i in range(rows)])

    def across_groups(value, step):
        return lax.ppermute(value, "items", [(i, i ^ step) for i in range(groups)])

    def array(*shape, dtype=F32):
        return jax.ShapeDtypeStruct(shape, dtype)

    sibling = across_cores(item_factor)
    asked = [item_blocks[0]] + [across_chips(item_blocks[0], step) for step in range(1, chips)]
    near = jnp.concatenate(asked, axis=0)
    far_users = across_groups(user_factor, groups // 2)
    held = pl.pallas_call(
        hold_kernel,
        out_shape=array(8, 128),
        in_specs=[SMEM],
        out_specs=VMEM,
        compiler_params=limit(4),
        cost_estimate=cost(4),
        name="hold",
    )(counts)

    served = pl.pallas_call(
        functools.partial(serve_kernel, chips, width),
        out_shape=[array(rank, slots * width)] * (chips - 1),
        in_specs=[SMEM] + [VMEM] * 2 + [ANY],
        out_specs=[VMEM] * (chips - 1),
        compiler_params=limit(4),
        cost_estimate=cost(1),
        name="serve",
    )(near, item_factor, sibling, held)
    messages = [across_chips(value, step + 1) for step, value in enumerate(served)]

    halves, spread, far_users = pl.pallas_call(
        prepare_kernel,
        out_shape=[
            array(slots, weeks, height, 2 * width, dtype=BF16),
            array(weeks, rank, height),
            array(rank, user_width),
        ],
        in_specs=[SMEM] + [VMEM] * 3 + [ANY],
        out_specs=[VMEM] * 3,
        compiler_params=limit(24),
        name="prepare",
    )(counts, tiles, week_factor, far_users, served[0])
    row_factors = {0: user_factor, groups // 2: far_users}
    step = groups // 4
    while step:
        row_factors |= {at ^ step: across_groups(v, step) for at, v in row_factors.items()}
        step //= 2

    even, odd = pl.pallas_call(
        functools.partial(mode1_kernel, groups),
        out_shape=[array(groups // 2, rank, user_width)] * 2,
        in_specs=[SMEM] * 3 + [VMEM] * (3 + chips),
        out_specs=[VMEM] * 2,
        scratch_shapes=[pltpu.VMEM((groups * user_width // height, rank, height), F32)],
        compiler_params=limit(8),
        cost_estimate=cost(1),
        name="mode1",
    )(
        counts,
        user_blocks[0],
        item_blocks[0],
        spread,
        halves,
        item_factor,
        sibling,
        *messages,
    )
    terms = pl.pallas_call(
        mode2_kernel,
        out_shape=array(rank, slots * width),
        in_specs=[SMEM] * 2 + [VMEM] * 2 + [ANY] + [VMEM] * groups,
        out_specs=VMEM,
        compiler_params=limit(8),
        cost_estimate=cost(2),
        name="mode2",
    )(
        counts,
        user_blocks[0],
        spread,
        halves,
        even,
        *(row_factors[step] for step in range(groups)),
    )
    near_terms = [terms] + [across_chips(terms, step) for step in range(1, chips)]
    own, other = pl.pallas_call(
        collect_kernel,
        out_shape=[array(*item_factor.shape)] * 2,
        in_specs=[SMEM] + [VMEM] * chips,
        out_specs=[VMEM] * 2,
        compiler_params=limit(4),
        name="collect",
    )(near, *near_terms)
    kept, sent, step = even, odd, 1
    while step < groups // 2:
        arrived = across_groups(sent, step)
        kept, sent = kept[0::2] + arrived[0::2], kept[1::2] + arrived[1::2]
        step *= 2
    users = pl.pallas_call(
        finish_users_kernel,
        out_shape=array(rank, user_width),
        in_specs=[VMEM] * 2,
        out_specs=VMEM,
        compiler_params=limit(4),
        cost_estimate=cost(4),
        name="finish_users",
    )(kept[0], across_groups(sent[0], step))
    m_items, m_users = pl.pallas_call(
        finish_items_kernel,
        out_shape=[array(*item_factor.shape), array(rank, user_width)],
        in_specs=[VMEM] * 3,
        out_specs=[VMEM] * 2,
        compiler_params=limit(4),
        name="finish_items",
    )(own, across_cores(other), users)
    return m_users, m_items


def solution(mesh):
    rows, groups = mesh.shape["users"], mesh.shape["items"]
    assert rows > 1 and rows & (rows - 1) == 0 and groups > 1 and groups & (groups - 1) == 0
    return jax.shard_map(
        functools.partial(on_device, (rows, groups)),
        mesh=mesh,
        in_specs=(
            P("users", "items", None, None, None, None),
            P("users", "items", None),
            P("users", "items", None),
            P("users", "items"),
            P(None, ("users", "items")),
            P(None, ("items", "users")),
            P(),
        ),
        out_specs=(P(None, ("users", "items")), P(None, ("items", "users"))),
        check_vma=False,
    )
```

```python
import functools

import jax
import jax.numpy as jnp
from jax import lax
from jax.experimental import pallas as pl
from jax.experimental.pallas import tpu as pltpu
from jax.sharding import PartitionSpec as P

F32 = jnp.float32
BF16 = jnp.bfloat16
ANY = pl.BlockSpec(memory_space=pl.ANY)
HBM = pl.BlockSpec(memory_space=pltpu.HBM)
SMEM = pl.BlockSpec(memory_space=pltpu.SMEM)
VMEM = pl.BlockSpec(memory_space=pltpu.VMEM)


def columns(block, width):
    return pl.ds(pl.multiple_of(block * width, width), width)


def split(value):
    high = value.astype(BF16)
    return high, (value - high.astype(F32)).astype(BF16)


def hold_kernel(done):
    done[...] = jnp.zeros_like(done)


def prepare_kernel(count_ref, tiles, week_factor, users, _, halves, spread, users_out):
    weeks, width = tiles.shape[1], tiles.shape[3]
    users_out[...] = users[...]
    weeks_t = week_factor[...].T
    for week in range(weeks):
        spread[week] = jnp.broadcast_to(weeks_t[:, week : week + 1], spread.shape[1:])

    def work(slot, carry):
        def one(week, inner):
            high, low = split(tiles[slot, week])
            halves[slot, week, :, :width] = high
            halves[slot, week, :, width:] = low
            return inner

        return lax.fori_loop(0, weeks, one, carry, unroll=8)

    lax.fori_loop(0, count_ref[0, 0], work, 0)


def serve_kernel(chips, width, requests, own, sibling, _, *messages):
    me = lax.axis_index("users")
    per_device = own.shape[1] // width
    for step in range(1, chips):
        for slot in range(requests.shape[1]):
            index = requests[step, slot]
            device = index // per_device
            place = columns(index % per_device, width)
            for owner, source in ((me, own), (me ^ 1, sibling)):

                @pl.when(device == owner)
                def _():
                    messages[step - 1][:, slot * width : (slot + 1) * width] = source[:, place]


def quarters(sums, size):
    total = pltpu.matmul_pop(sums[0])
    for other in sums[1:]:
        total += pltpu.matmul_pop(other)
    half = total[: total.shape[0] // 2] + total[total.shape[0] // 2 :]
    return half[:, :size] + half[:, size:]


def multiply(sums, at, left, right, transpose):
    unit, stage = at % len(sums), at // len(sums) % 2
    pltpu.matmul_push_rhs(right, stage, unit, transpose=transpose)
    pltpu.matmul_acc_lhs(sums[unit], left, load_staged_rhs=stage)


def user_term(spread, items, tile, sums):
    weeks, height, width = tile.shape
    width //= 2
    for at in range(weeks // 2):
        left, right = [], []
        for part in (2 * at, 2 * at + 1):
            left.append(jnp.concatenate(split(spread[part] * items), axis=0))
            right.append(jnp.concatenate([tile[part, :, :width], tile[part, :, width:]], axis=0))
        left, right = jnp.concatenate(left, axis=1), jnp.concatenate(right, axis=1)
        multiply(sums, at, left, right, True)
    return quarters(sums, height)


def item_term(spread, users, tile, sums):
    weeks, height, width = tile.shape
    for at in range(weeks // 2):
        left = [
            jnp.concatenate(split(spread[part] * users), axis=0) for part in (2 * at, 2 * at + 1)
        ]
        right = tile[2 * at : 2 * at + 2].reshape(2 * height, width)
        multiply(sums, at, jnp.concatenate(left, axis=1), right, False)
    return quarters(sums, width // 2)


def mode1_kernel(units, count_ref, users_ref, items_ref, spread, tiles, own, sibling, *refs):
    *messages, even, odd = refs
    height, width = tiles.shape[2], tiles.shape[3] // 2
    me = lax.axis_index("users")
    column = lax.axis_index("items")
    per_device = own.shape[1] // width
    kept = even.shape[2] // height
    even[...] = jnp.zeros_like(even)
    odd[...] = jnp.zeros_like(odd)

    def work(slot, carry):
        index = items_ref[0, slot]
        device = index // per_device
        place = columns(index % per_device, width)
        items = jnp.where(device == me, own[:, place], sibling[:, place])
        source = (device // 2) ^ (me // 2)
        here = columns(slot, width)
        for step, message in enumerate(messages):
            items = jnp.where(source == step + 1, message[:, here], items)
        term = pl.run_scoped(
            lambda *held: user_term(spread, items, tiles.at[slot], held), *units
        )
        block = users_ref[0, slot]
        step = (block // kept) ^ column
        place = columns(block % kept, height)
        for parity, target in enumerate((even, odd)):

            @pl.when(step % 2 == parity)
            def _():
                target[step // 2, :, place] += term

        return carry

    lax.fori_loop(0, count_ref[0, 0], work, 0)


def mode2_kernel(units, count_ref, users_ref, spread, tiles, _, *refs):
    *factors, terms = refs
    height, width = tiles.shape[2], tiles.shape[3] // 2
    column = lax.axis_index("items")
    kept = factors[0].shape[1] // height
    terms[...] = jnp.zeros_like(terms)

    def work(slot, carry):
        block = users_ref[0, slot]
        source = (block // kept) ^ column
        place = columns(block % kept, height)
        users = factors[0][:, place]
        for step in range(1, len(factors)):
            users = jnp.where(source == step, factors[step][:, place], users)
        terms[:, columns(slot, width)] = pl.run_scoped(
            lambda *held: item_term(spread, users, tiles.at[slot], held), *units
        )
        return carry

    lax.fori_loop(0, count_ref[0, 0], work, 0)


def collect_kernel(ids, *refs):
    *terms, own, other = refs
    slots = ids.shape[1]
    width = terms[0].shape[1] // slots
    per_device = own.shape[1] // width
    me = lax.axis_index("users")
    own[...] = jnp.zeros_like(own)
    other[...] = jnp.zeros_like(other)
    for step, term in enumerate(terms):
        for slot in range(slots):
            index = ids[step, slot]
            device = index // per_device
            place = columns(index % per_device, width)
            for owner, target in ((me, own), (me ^ 1, other)):

                @pl.when(device == owner)
                def _():
                    target[:, place] += term[:, slot * width : (slot + 1) * width]


def finish_users_kernel(kept, arrived, total):
    total[...] = kept[...] + arrived[...]


def finish_items_kernel(own, arrived, users, items_out, users_out):
    users_out[...] = users[...]
    items_out[...] = own[...] + arrived[...]


def on_device(mesh, tiles, user_blocks, item_blocks, counts, user_factor, item_factor, week_factor):
    rows, groups = mesh.shape["users"], mesh.shape["items"]
    chips = rows // 2
    tiles = tiles[0, 0]
    slots, weeks, height, width = tiles.shape
    rank = week_factor.shape[1]
    user_width = user_factor.shape[1]

    def limit(mebibytes):
        return pltpu.CompilerParams(vmem_limit_bytes=mebibytes << 20)

    def cost(times):
        return pl.CostEstimate(
            flops=int(times * 8 * slots * weeks * height * width * rank),
            bytes_accessed=int(times * 4 * slots * weeks * height * width),
            transcendentals=0,
        )

    with jax.sharding.use_abstract_mesh(mesh.abstract_mesh):
        units = [pltpu.ACC(unit)((2 * rank, 2 * width), F32) for unit in range(2)]

    def across_chips(value, step):
        return lax.ppermute(value, "users", [(i, i ^ (2 * step)) for i in range(rows)])

    def across_cores(value):
        return lax.ppermute(value, "users", [(i, i ^ 1) for i in range(rows)])

    def across_groups(value, step):
        return lax.ppermute(value, "items", [(i, i ^ step) for i in range(groups)])

    def array(*shape, dtype=F32):
        return jax.ShapeDtypeStruct(shape, dtype)

    sibling = across_cores(item_factor)
    asked = [item_blocks[0]] + [across_chips(item_blocks[0], step) for step in range(1, chips)]
    near = jnp.concatenate(asked, axis=0)
    far_users = across_groups(user_factor, groups // 2)
    held = pl.pallas_call(
        hold_kernel,
        out_shape=array(8, 128),
        out_specs=VMEM,
        compiler_params=limit(4),
        cost_estimate=cost(4),
        name="hold",
    )()

    served = pl.pallas_call(
        functools.partial(serve_kernel, chips, width),
        out_shape=[array(rank, slots * width)] * (chips - 1),
        in_specs=[SMEM] + [VMEM] * 2 + [ANY],
        out_specs=[VMEM] * (chips - 1),
        compiler_params=limit(4),
        cost_estimate=cost(1),
        name="serve",
    )(near, item_factor, sibling, held)
    messages = [across_chips(value, step + 1) for step, value in enumerate(served)]

    halves, spread, far_users = pl.pallas_call(
        prepare_kernel,
        out_shape=[
            array(slots, weeks, height, 2 * width, dtype=BF16),
            array(weeks, rank, height),
            array(rank, user_width),
        ],
        in_specs=[SMEM] + [VMEM] * 3 + [ANY],
        out_specs=[VMEM] * 3,
        compiler_params=limit(24),
        name="prepare",
    )(counts, tiles, week_factor, far_users, served[0])
    row_factors = {0: user_factor, groups // 2: far_users}
    step = groups // 4
    while step:
        row_factors |= {at ^ step: across_groups(v, step) for at, v in row_factors.items()}
        step //= 2

    even, odd = pl.pallas_call(
        functools.partial(mode1_kernel, units),
        out_shape=[array(groups // 2, rank, user_width)] * 2,
        in_specs=[SMEM] * 3 + [VMEM] * (3 + chips),
        out_specs=[VMEM] * 2,
        compiler_params=limit(8),
        cost_estimate=cost(1),
        name="mode1",
    )(
        counts,
        user_blocks[0],
        item_blocks[0],
        spread,
        halves,
        item_factor,
        sibling,
        *messages,
    )
    terms = pl.pallas_call(
        functools.partial(mode2_kernel, units),
        out_shape=array(rank, slots * width),
        in_specs=[SMEM] * 2 + [VMEM] * 2 + [ANY] + [VMEM] * groups,
        out_specs=VMEM,
        compiler_params=limit(8),
        cost_estimate=cost(2),
        name="mode2",
    )(
        counts,
        user_blocks[0],
        spread,
        halves,
        even,
        *(row_factors[step] for step in range(groups)),
    )
    far_first = {step: across_chips(terms, step) for step in reversed(range(1, chips))}
    near_terms = [terms] + [far_first[step] for step in range(1, chips)]
    own, other = pl.pallas_call(
        collect_kernel,
        out_shape=[array(*item_factor.shape)] * 2,
        in_specs=[SMEM] + [VMEM] * chips,
        out_specs=[VMEM] * 2,
        compiler_params=limit(4),
        name="collect",
    )(near, *near_terms)
    kept, sent, step = even, odd, 1
    while step < groups // 2:
        arrived = across_groups(sent, step)
        kept, sent = kept[0::2] + arrived[0::2], kept[1::2] + arrived[1::2]
        step *= 2
    users = pl.pallas_call(
        finish_users_kernel,
        out_shape=array(rank, user_width),
        in_specs=[VMEM] * 2,
        out_specs=VMEM,
        compiler_params=limit(4),
        cost_estimate=cost(4),
        name="finish_users",
    )(kept[0], across_groups(sent[0], step))
    m_items, m_users = pl.pallas_call(
        finish_items_kernel,
        out_shape=[array(*item_factor.shape), array(rank, user_width)],
        in_specs=[VMEM] * 3,
        out_specs=[VMEM] * 2,
        compiler_params=limit(4),
        name="finish_items",
    )(own, across_cores(other), users)
    return m_users, m_items


def solution(mesh):
    rows, groups = mesh.shape["users"], mesh.shape["items"]
    assert rows > 1 and rows & (rows - 1) == 0 and groups > 1 and groups & (groups - 1) == 0
    return jax.shard_map(
        functools.partial(on_device, mesh),
        mesh=mesh,
        in_specs=(
            P("users", "items", None, None, None, None),
            P("users", "items", None),
            P("users", "items", None),
            P("users", "items"),
            P(None, ("users", "items")),
            P(None, ("items", "users")),
            P(),
        ),
        out_specs=(P(None, ("users", "items")), P(None, ("items", "users"))),
        check_vma=False,
    )
```

```python
import functools

import jax
import jax.numpy as jnp
from jax import lax
from jax.experimental import pallas as pl
from jax.experimental.pallas import tpu as pltpu
from jax.sharding import PartitionSpec as P

F32 = jnp.float32
BF16 = jnp.bfloat16
ANY = pl.BlockSpec(memory_space=pl.ANY)
HBM = pl.BlockSpec(memory_space=pltpu.HBM)
SMEM = pl.BlockSpec(memory_space=pltpu.SMEM)
VMEM = pl.BlockSpec(memory_space=pltpu.VMEM)


def columns(block, width):
    return pl.ds(pl.multiple_of(block * width, width), width)


def split(value):
    high = value.astype(BF16)
    return high, (value - high.astype(F32)).astype(BF16)


def hold_kernel(done):
    done[...] = jnp.zeros_like(done)


def prepare_kernel(count_ref, tiles, week_factor, users, _, halves, spread, users_out):
    weeks, width = tiles.shape[1], tiles.shape[3]
    users_out[...] = users[...]
    weeks_t = week_factor[...].T
    for week in range(weeks):
        spread[week] = jnp.broadcast_to(weeks_t[:, week : week + 1], spread.shape[1:])

    def work(slot, carry):
        def one(week, inner):
            high, low = split(tiles[slot, week])
            halves[slot, week, :, :width] = high
            halves[slot, week, :, width:] = low
            return inner

        return lax.fori_loop(0, weeks, one, carry, unroll=16)

    lax.fori_loop(0, count_ref[0, 0], work, 0)


def serve_kernel(chips, width, requests, own, sibling, _, *messages):
    me = lax.axis_index("users")
    per_device = own.shape[1] // width
    for step in range(1, chips):
        for slot in range(requests.shape[1]):
            index = requests[step, slot]
            device = index // per_device
            place = columns(index % per_device, width)
            for owner, source in ((me, own), (me ^ 1, sibling)):

                @pl.when(device == owner)
                def _():
                    messages[step - 1][:, slot * width : (slot + 1) * width] = source[:, place]


def quarters(sums, size):
    total = pltpu.matmul_pop(sums[0])
    for other in sums[1:]:
        total += pltpu.matmul_pop(other)
    half = total[: total.shape[0] // 2] + total[total.shape[0] // 2 :]
    return half[:, :size] + half[:, size:]


def multiply(sums, at, left, right, transpose):
    unit, stage = at % len(sums), at // len(sums) % 2
    pltpu.matmul_push_rhs(right, stage, unit, transpose=transpose)
    pltpu.matmul_acc_lhs(sums[unit], left, load_staged_rhs=stage)


def user_term(spread, items, tile, sums):
    weeks, height, width = tile.shape
    width //= 2
    for at in range(weeks // 2):
        left, right = [], []
        for part in (2 * at, 2 * at + 1):
            left.append(jnp.concatenate(split(spread[part] * items), axis=0))
            right.append(jnp.concatenate([tile[part, :, :width], tile[part, :, width:]], axis=0))
        left, right = jnp.concatenate(left, axis=1), jnp.concatenate(right, axis=1)
        multiply(sums, at, left, right, True)
    return quarters(sums, height)


def item_term(spread, users, tile, sums):
    weeks, height, width = tile.shape
    for at in range(weeks // 2):
        left = [
            jnp.concatenate(split(spread[part] * users), axis=0) for part in (2 * at, 2 * at + 1)
        ]
        right = tile[2 * at : 2 * at + 2].reshape(2 * height, width)
        multiply(sums, at, jnp.concatenate(left, axis=1), right, False)
    return quarters(sums, width // 2)


def mode1_kernel(units, count_ref, users_ref, items_ref, spread, tiles, own, sibling, *refs):
    *messages, even, odd = refs
    height, width = tiles.shape[2], tiles.shape[3] // 2
    me = lax.axis_index("users")
    column = lax.axis_index("items")
    per_device = own.shape[1] // width
    kept = even.shape[2] // height
    even[...] = jnp.zeros_like(even)
    odd[...] = jnp.zeros_like(odd)

    def work(slot, carry):
        index = items_ref[0, slot]
        device = index // per_device
        place = columns(index % per_device, width)
        items = jnp.where(device == me, own[:, place], sibling[:, place])
        source = (device // 2) ^ (me // 2)
        here = columns(slot, width)
        for step, message in enumerate(messages):
            items = jnp.where(source == step + 1, message[:, here], items)
        term = pl.run_scoped(
            lambda *held: user_term(spread, items, tiles.at[slot], held), *units
        )
        block = users_ref[0, slot]
        step = (block // kept) ^ column
        place = columns(block % kept, height)
        for parity, target in enumerate((even, odd)):

            @pl.when(step % 2 == parity)
            def _():
                target[step // 2, :, place] += term

        return carry

    lax.fori_loop(0, count_ref[0, 0], work, 0)


def mode2_kernel(units, count_ref, users_ref, spread, tiles, _, *refs):
    *factors, terms = refs
    height, width = tiles.shape[2], tiles.shape[3] // 2
    column = lax.axis_index("items")
    kept = factors[0].shape[1] // height
    terms[...] = jnp.zeros_like(terms)

    def work(slot, carry):
        block = users_ref[0, slot]
        source = (block // kept) ^ column
        place = columns(block % kept, height)
        users = factors[0][:, place]
        for step in range(1, len(factors)):
            users = jnp.where(source == step, factors[step][:, place], users)
        terms[:, columns(slot, width)] = pl.run_scoped(
            lambda *held: item_term(spread, users, tiles.at[slot], held), *units
        )
        return carry

    lax.fori_loop(0, count_ref[0, 0], work, 0)


def collect_kernel(ids, *refs):
    *terms, own, other = refs
    slots = ids.shape[1]
    width = terms[0].shape[1] // slots
    per_device = own.shape[1] // width
    me = lax.axis_index("users")
    own[...] = jnp.zeros_like(own)
    other[...] = jnp.zeros_like(other)
    for step, term in enumerate(terms):
        for slot in range(slots):
            index = ids[step, slot]
            device = index // per_device
            place = columns(index % per_device, width)
            for owner, target in ((me, own), (me ^ 1, other)):

                @pl.when(device == owner)
                def _():
                    target[:, place] += term[:, slot * width : (slot + 1) * width]


def finish_users_kernel(kept, arrived, total):
    total[...] = kept[...] + arrived[...]


def finish_items_kernel(own, arrived, users, items_out, users_out):
    users_out[...] = users[...]
    items_out[...] = own[...] + arrived[...]


def on_device(mesh, tiles, user_blocks, item_blocks, counts, user_factor, item_factor, week_factor):
    rows, groups = mesh.shape["users"], mesh.shape["items"]
    chips = rows // 2
    tiles = tiles[0, 0]
    slots, weeks, height, width = tiles.shape
    rank = week_factor.shape[1]
    user_width = user_factor.shape[1]

    def limit(mebibytes):
        return pltpu.CompilerParams(vmem_limit_bytes=mebibytes << 20)

    def cost(times):
        return pl.CostEstimate(
            flops=int(times * 8 * slots * weeks * height * width * rank),
            bytes_accessed=int(times * 4 * slots * weeks * height * width),
            transcendentals=0,
        )

    with jax.sharding.use_abstract_mesh(mesh.abstract_mesh):
        units = [pltpu.ACC(unit)((2 * rank, 2 * width), F32) for unit in range(2)]

    def across_chips(value, step):
        return lax.ppermute(value, "users", [(i, i ^ (2 * step)) for i in range(rows)])

    def across_cores(value):
        return lax.ppermute(value, "users", [(i, i ^ 1) for i in range(rows)])

    def across_groups(value, step):
        return lax.ppermute(value, "items", [(i, i ^ step) for i in range(groups)])

    def array(*shape, dtype=F32):
        return jax.ShapeDtypeStruct(shape, dtype)

    sibling = across_cores(item_factor)
    asked = [item_blocks[0]] + [across_chips(item_blocks[0], step) for step in range(1, chips)]
    near = jnp.concatenate(asked, axis=0)
    far_users = across_groups(user_factor, groups // 2)
    held = pl.pallas_call(
        hold_kernel,
        out_shape=array(8, 128),
        out_specs=VMEM,
        compiler_params=limit(4),
        cost_estimate=cost(4),
        name="hold",
    )()

    served = pl.pallas_call(
        functools.partial(serve_kernel, chips, width),
        out_shape=[array(rank, slots * width)] * (chips - 1),
        in_specs=[SMEM] + [VMEM] * 2 + [ANY],
        out_specs=[VMEM] * (chips - 1),
        compiler_params=limit(4),
        cost_estimate=cost(1),
        name="serve",
    )(near, item_factor, sibling, held)
    messages = [across_chips(value, step + 1) for step, value in enumerate(served)]

    halves, spread, far_users = pl.pallas_call(
        prepare_kernel,
        out_shape=[
            array(slots, weeks, height, 2 * width, dtype=BF16),
            array(weeks, rank, height),
            array(rank, user_width),
        ],
        in_specs=[SMEM] + [VMEM] * 3 + [ANY],
        out_specs=[VMEM] * 3,
        compiler_params=limit(24),
        name="prepare",
    )(counts, tiles, week_factor, far_users, served[0])
    row_factors = {0: user_factor, groups // 2: far_users}
    step = groups // 4
    while step:
        row_factors |= {at ^ step: across_groups(v, step) for at, v in row_factors.items()}
        step //= 2

    even, odd = pl.pallas_call(
        functools.partial(mode1_kernel, units),
        out_shape=[array(groups // 2, rank, user_width)] * 2,
        in_specs=[SMEM] * 3 + [VMEM] * (3 + chips),
        out_specs=[VMEM] * 2,
        compiler_params=limit(8),
        cost_estimate=cost(1),
        name="mode1",
    )(
        counts,
        user_blocks[0],
        item_blocks[0],
        spread,
        halves,
        item_factor,
        sibling,
        *messages,
    )
    terms = pl.pallas_call(
        functools.partial(mode2_kernel, units),
        out_shape=array(rank, slots * width),
        in_specs=[SMEM] * 2 + [VMEM] * 2 + [ANY] + [VMEM] * groups,
        out_specs=VMEM,
        compiler_params=limit(8),
        cost_estimate=cost(2),
        name="mode2",
    )(
        counts,
        user_blocks[0],
        spread,
        halves,
        even,
        *(row_factors[step] for step in range(groups)),
    )
    far_first = {step: across_chips(terms, step) for step in reversed(range(1, chips))}
    near_terms = [terms] + [far_first[step] for step in range(1, chips)]
    own, other = pl.pallas_call(
        collect_kernel,
        out_shape=[array(*item_factor.shape)] * 2,
        in_specs=[SMEM] + [VMEM] * chips,
        out_specs=[VMEM] * 2,
        compiler_params=limit(4),
        name="collect",
    )(near, *near_terms)
    kept, sent, step = even, odd, 1
    while step < groups // 2:
        arrived = across_groups(sent, step)
        kept, sent = kept[0::2] + arrived[0::2], kept[1::2] + arrived[1::2]
        step *= 2
    users = pl.pallas_call(
        finish_users_kernel,
        out_shape=array(rank, user_width),
        in_specs=[VMEM] * 2,
        out_specs=VMEM,
        compiler_params=limit(4),
        cost_estimate=cost(4),
        name="finish_users",
    )(kept[0], across_groups(sent[0], step))
    m_items, m_users = pl.pallas_call(
        finish_items_kernel,
        out_shape=[array(*item_factor.shape), array(rank, user_width)],
        in_specs=[VMEM] * 3,
        out_specs=[VMEM] * 2,
        compiler_params=limit(4),
        name="finish_items",
    )(own, across_cores(other), users)
    return m_users, m_items


def solution(mesh):
    rows, groups = mesh.shape["users"], mesh.shape["items"]
    assert rows > 1 and rows & (rows - 1) == 0 and groups > 1 and groups & (groups - 1) == 0
    return jax.shard_map(
        functools.partial(on_device, mesh),
        mesh=mesh,
        in_specs=(
            P("users", "items", None, None, None, None),
            P("users", "items", None),
            P("users", "items", None),
            P("users", "items"),
            P(None, ("users", "items")),
            P(None, ("items", "users")),
            P(),
        ),
        out_specs=(P(None, ("users", "items")), P(None, ("items", "users"))),
        check_vma=False,
    )
```
